32 devices in a mesh: grp: 2 (over y), ctx: 4 (over z), head: 4 (over x, core).
Axes of the slice: x: 2, y: 2, z: 4, core: 2. Of those that a mesh axis runs over, the one named last changes fastest.
Arguments:
- main_queries: bfloat16 [1024, 128, 576], P(('grp', 'ctx'), 'head'), parts along dimension 0, may hold values from -6 to 6
- latent_keys: bfloat16 [32768, 576], P(('grp', 'ctx')), parts along dimension 0, may hold values from -6 to 6
- lse: float32 [1024, 128], P(('grp', 'ctx'), 'head'), parts along dimension 0, may hold values from 6 to 10
- index_queries: bfloat16 [1024, 64, 128], P(('grp', 'ctx'), 'head'), parts along dimension 0, may hold values from -9 to 9
- index_keys: bfloat16 [32768, 128], P(('grp', 'ctx')), parts along dimension 0, may hold values from -1 to 1
- head_weights: float32 [1024, 64], P(('grp', 'ctx'), 'head'), parts along dimension 0, may hold values from -0.1 to 0.5
- loss_cotangent: float32 [1024], P(('grp', 'ctx')), parts along dimension 0, may hold values from 32 to 128
- block_ids: int32 [1024, 32], P(('grp', 'ctx')), parts along dimension 0, may hold values from 0 to 255, as said below
Outputs:
- d_index_queries: bfloat16 [1024, 64, 128], P(('grp', 'ctx'), 'head'), parts along dimension 0
- d_head_weights: float32 [1024, 64], P(('grp', 'ctx'), 'head'), parts along dimension 0
- d_index_keys: float32 [32768, 128], P(('grp', 'ctx')), parts along dimension 0
The draws below stay inside these ranges and needn't reach their ends.
There are 2 independent parts, one for each index of `grp`. The reference program is written for one: setup_inputs(seed, part) draws one part's arguments, and reference() takes and returns one part's arrays. A program takes and returns all parts, laid end to end along the dimension named above; each array names one. Nothing has to cross between parts.
Inputs may be any that keep to these rules, and one draw needn't show every extreme that they name: `block_ids`: each row names 32 different blocks, none of which starts after the query's position. The 128 rows of one ctx device name exactly 64 distinct blocks together; at most 32 of them lie among the keys of any one ctx device, and exactly 32 among the keys of the last ctx device.
All inputs are finite; a program needn't handle non-finite values.
Results may differ from the reference program's by a relative error of at most 0.0048.
Values may be sent and summed in bfloat16 or wider, within the bound.
A program may use at most 192 MiB of HBM per device.

```python
import jax
import jax.numpy as jnp
from jax import lax

DL = 576
HM = 128
IH = 64
DI = 128
BLK = 64
TOPB = 32
UB = 64
QD = 128
KD = 4096
QUERIES = 512
KEYS = 16384


def base_index_keys(key):
    return jnp.clip(jax.random.normal(key, (KEYS, DI), jnp.float32), -4.0, 4.0) * DI ** (-0.5)


def draw_index_keys(key, part):
    base = base_index_keys(key)
    return base.astype(jnp.bfloat16)


def draw_index_queries(key, part):
    key = jax.random.fold_in(key, 12)
    queries = jnp.clip(jax.random.normal(key, (QUERIES, IH, DI), jnp.float32), -6.0, 6.0)
    return queries.astype(jnp.bfloat16)


def draw_block_ids(key, part):
    key = jax.random.fold_in(key, 13)
    ctx_count = QUERIES // QD
    owner_blocks = KD // BLK
    own_count = QD // BLK
    slot_count = 2 * UB // ctx_count
    window = (KEYS - QUERIES) // BLK
    last_start = (ctx_count - 1) * owner_blocks

    def one_device(dev_key, device):
        first_key, second_key, third_key, fourth_key = jax.random.split(dev_key, 4)
        diagonal = window + device * own_count + jnp.arange(own_count, dtype=jnp.int32)
        earlier = last_start + jax.random.permutation(first_key, window - last_start)[:slot_count - own_count]
        picked = jax.random.permutation(second_key, (ctx_count - 1) * slot_count)[:UB - slot_count]
        owner = picked // slot_count
        slot_index = picked % slot_count
        shuffles = jax.vmap(lambda sub_key: jax.random.permutation(sub_key, owner_blocks))(jax.random.split(third_key, ctx_count - 1))
        distant = owner * owner_blocks + shuffles[owner, slot_index]
        block_pool = jnp.concatenate([diagonal, earlier.astype(jnp.int32), distant.astype(jnp.int32)])
        row_index = jnp.arange(QD, dtype=jnp.int32)
        own_block = row_index // BLK
        pool_index = jnp.arange(UB, dtype=jnp.int32)
        noise = jax.random.randint(fourth_key, (QD, UB), 0, 1 << 20)
        rest_count = UB - own_count
        forced = pool_index[None, :] - own_count == row_index[:, None] % rest_count
        ranking = noise * UB + pool_index[None, :] + jnp.where(forced, 1 << 28, 0)
        diag_rank = jnp.where(pool_index[None, :] <= own_block[:, None], (1 << 29) + pool_index[None, :], -(1 << 29))
        ranking = jnp.where(pool_index[None, :] < own_count, diag_rank, ranking)
        ranked = lax.top_k(ranking, TOPB)[1]
        return block_pool[ranked]
    chosen = jax.vmap(one_device)(jax.random.split(key, ctx_count), jnp.arange(ctx_count, dtype=jnp.int32))
    return chosen.reshape(QUERIES, TOPB).astype(jnp.int32)


def block_scale(stream_key, shape, pieces, low, top_value):
    def one(axis_at, parts):
        heights = jax.random.uniform(jax.random.fold_in(jax.random.fold_in(stream_key, 6), axis_at), (parts,), jnp.float32, low / len(pieces), top_value / len(pieces))
        return jnp.repeat(jnp.exp(heights), shape[axis_at] // parts).reshape((-1,) + (1,) * (len(shape) - axis_at - 1))

    level = one(*pieces[0])
    for cut in pieces[1:]:
        level = level * one(*cut)
    return level


def scatter_about(own_key, extent, width, most, shards=(), kind=jnp.bfloat16):
    result = jax.random.normal(own_key, extent, jnp.float32) * width
    if len(shards) > 0:
        result = block_scale(own_key, extent, shards, -0.22, 0.18) * result
    return jnp.clip(result, min=-most, max=most).astype(kind)


def setup_inputs(seed: int = 0, part: int = 0) -> dict:
    key_of = jax.random.split(jax.random.key(seed), 9)
    part_splits = jax.random.split(jax.random.fold_in(key_of[8], part), 9)
    main_queries = scatter_about(part_splits[0], (QUERIES, HM, DL), 1.0, 6.0, ((0, 4), (1, 4)))
    latent_keys = scatter_about(part_splits[1], (KEYS, DL), 1.0, 6.0, ((0, 4),))
    lse = jnp.clip(6.0 + 4.0 * jax.random.uniform(part_splits[2], (QUERIES, HM), jnp.float32) ** block_scale(part_splits[2], (QUERIES, HM), ((0, 4), (1, 4)), -0.2, 0.2), 6.0, 10.0)
    index_queries = draw_index_queries(jax.random.fold_in(jax.random.fold_in(key_of[8], part), 71), part)
    index_keys = draw_index_keys(jax.random.fold_in(jax.random.fold_in(key_of[8], part), 71), part)
    head_weights = jnp.clip(-0.1 + 0.6 * jax.random.uniform(part_splits[5], (QUERIES, IH), jnp.float32) ** block_scale(part_splits[5], (QUERIES, IH), ((0, 4), (1, 4)), -0.2, 0.2), -0.1, 0.5)
    loss_cotangent = jnp.clip(32.0 + 96.0 * jax.random.uniform(part_splits[6], (QUERIES,), jnp.float32) ** block_scale(part_splits[6], (QUERIES,), ((0, 4),), -0.2, 0.2), 32.0, 128.0)
    block_ids = draw_block_ids(jax.random.fold_in(jax.random.fold_in(key_of[8], part), 71), part)
    return {"main_queries": main_queries, "latent_keys": latent_keys, "lse": lse, "index_queries": index_queries, "index_keys": index_keys, "head_weights": head_weights, "loss_cotangent": loss_cotangent, "block_ids": block_ids}


ATTN_SCALE = 192.0 ** -0.5


def smooth_gate(value):
    return jnp.maximum(value, 0.0)


def smooth_slope(value):
    return jnp.where(value > 0.0, 1.0, 0.0)


def reference(main_queries, latent_keys, lse, index_queries, index_keys, head_weights, loss_cotangent, block_ids):
    query_total = main_queries.shape[0]
    key_total = latent_keys.shape[0]
    lat_blocks = latent_keys.reshape(key_total // BLK, BLK, DL)
    idx_blocks = index_keys.reshape(key_total // BLK, BLK, DI)
    offsets = jnp.arange(BLK, dtype=jnp.int32)

    def one_query(query_row, chosen_ids, queries, logsum, index_query, weights, cotangent):
        block_keys = lat_blocks[chosen_ids].reshape(TOPB * BLK, DL)
        index_rows = idx_blocks[chosen_ids].reshape(TOPB * BLK, DI)
        key_pos = (chosen_ids[:, None] * BLK + offsets[None, :]).reshape(-1).astype(jnp.int32)
        visible = key_pos <= (key_total - query_total) + query_row
        scores = jnp.dot(queries, block_keys.T, preferred_element_type=jnp.float32) * ATTN_SCALE
        main_prob = jnp.where(visible[None, :], jnp.exp(scores - logsum[:, None]), 0.0)
        head_mass = jnp.sum(main_prob, axis=0)
        target = head_mass / jnp.sum(head_mass)
        index_pre = jnp.dot(index_query, index_rows.T, preferred_element_type=jnp.float32)
        activated = smooth_gate(index_pre)
        index_score = jnp.sum(weights[:, None] * activated, axis=0)
        row_top = jnp.max(jnp.where(visible, index_score, -1e30))
        exponent = jnp.where(visible, jnp.exp(index_score - row_top), 0.0)
        score_grad = cotangent * (exponent / jnp.sum(exponent) - target)
        d_weights = jnp.sum(score_grad[None, :] * activated, axis=1)
        pre_grad = (score_grad[None, :] * weights[:, None] * smooth_slope(index_pre)).astype(jnp.bfloat16)
        d_queries = jnp.dot(pre_grad, index_rows, preferred_element_type=jnp.float32).astype(jnp.bfloat16)
        key_grad = jnp.dot(pre_grad.T, index_query, preferred_element_type=jnp.float32)
        return d_queries, d_weights, key_grad, key_pos

    group_size = 8
    row_index = jnp.arange(query_total, dtype=jnp.int32).reshape(-1, group_size)

    def step(key_sum, scanned):
        d_queries, d_weights, key_grad, key_pos = jax.vmap(one_query)(*scanned)
        key_sum = key_sum.at[key_pos.reshape(-1)].add(key_grad.reshape(-1, DI))
        return key_sum, (d_queries, d_weights)

    scanned = (row_index,
               block_ids.reshape(-1, group_size, TOPB),
               main_queries.reshape(-1, group_size, HM, DL),
               lse.reshape(-1, group_size, HM),
               index_queries.reshape(-1, group_size, IH, DI),
               head_weights.reshape(-1, group_size, IH),
               loss_cotangent.reshape(-1, group_size))
    key_sum, (dq_all, dw_all) = lax.scan(step, jnp.zeros((key_total, DI), jnp.float32), scanned)
    return dq_all.reshape(query_total, IH, DI), dw_all.reshape(query_total, IH), key_sum
```

```python
import functools
import math

import jax
import jax.numpy as jnp
from jax import lax
from jax.experimental import pallas as pl
from jax.experimental.pallas import tpu as pltpu
from jax.sharding import PartitionSpec as P

BLK = 64
UB = 64
GB = 8
ATTN_SCALE = 192.0 ** (-0.5)
LOG2E = math.log2(math.e)
MESH = pl.DeviceIdType.MESH
VMEM_LIMIT = 56 * 1024 * 1024
F32 = jnp.float32
BF16 = jnp.bfloat16


def place():
    head = lax.axis_index("head")
    x, core = head // 2, lax.rem(head, 2)
    return head, x, core, x * 2 + 1 - core


def greet(peers):
    barrier = pltpu.get_barrier_semaphore()
    for peer in peers:
        pl.semaphore_signal(barrier, inc=1, device_id=peer, device_id_type=MESH)
    pl.semaphore_wait(barrier, len(peers))


def remote(src, dst, send, recv, peer):
    return pltpu.make_async_remote_copy(
        src_ref=src, dst_ref=dst, send_sem=send, recv_sem=recv,
        device_id=peer, device_id_type=MESH,
    )


def fetch_kernel(n_ctx, n_head, lat_mine, idx_mine, lat_own, idx_own, lat_got, idx_got,
                 own_sem, recv_sem, s_ctx, s_x, s_core):
    me = lax.axis_index("ctx")
    head, x, core, partner = place()
    n_x = n_head // 2
    others = [lax.rem(me + k, n_ctx) for k in range(1, n_ctx)]
    xs = [lax.rem(x + k, n_x) for k in range(1, n_x)]
    greet([{"ctx": o} for o in others] + [{"head": v * 2 + core} for v in xs] + [{"head": partner}])
    mine, own, got = (idx_mine, lat_mine), (idx_own, lat_own), (idx_got, lat_got)
    pending = []
    for a in range(2):
        for i, o in enumerate(others):
            c = remote(mine[a].at[o], got[a].at[me, head], s_ctx.at[a, i],
                       recv_sem.at[a, me, head], {"ctx": o})
            c.start()
            pending.append(c)
    locals_ = []
    for a in range(2):
        c = pltpu.make_async_copy(own[a], got[a].at[me], own_sem.at[a])
        c.start()
        locals_.append(c)

    def arrived(a, o, h):
        remote(got[a].at[o, h], got[a].at[o, h], s_core.at[a, 0, 0], recv_sem.at[a, o, h],
               {"head": partner}).wait_recv()

    def forward(a, i, o, h, slot):
        c = remote(got[a].at[o, h], got[a].at[o, h], s_core.at[a, i, slot],
                   recv_sem.at[a, o, h], {"head": partner})
        c.start()
        pending.append(c)

    sources = [lax.rem(me + n_ctx - k, n_ctx) for k in range(1, n_ctx)]
    for a in range(2):
        for i, o in enumerate(sources):
            arrived(a, o, head)
            for j, v in enumerate(xs):
                c = remote(got[a].at[o, head], got[a].at[o, head], s_x.at[a, i, j],
                           recv_sem.at[a, o, head], {"head": v * 2 + core})
                c.start()
                pending.append(c)
            forward(a, i, o, head, 0)
    for a in range(2):
        for i, o in enumerate(sources):
            for j, v in enumerate(xs):
                arrived(a, o, v * 2 + core)
                forward(a, i, o, v * 2 + core, 1 + j)
    for a in range(2):
        for i, o in enumerate(sources):
            for v in [x] + xs:
                arrived(a, o, v * 2 + 1 - core)
    for c in pending:
        c.wait_send()
    for c in locals_:
        c.wait()


def fetch(n_ctx, n_head, lat_mine, idx_mine, lat_own, idx_own):
    per, _, wl = lat_mine.shape[1:]
    wi = idx_mine.shape[-1]
    n_x = n_head // 2
    dma = pltpu.SemaphoreType.DMA
    return pl.pallas_call(
        functools.partial(fetch_kernel, n_ctx, n_head),
        out_shape=(
            jax.ShapeDtypeStruct((n_ctx, n_head, per, BLK, wl), BF16),
            jax.ShapeDtypeStruct((n_ctx, n_head, per, BLK, wi), BF16),
        ),
        in_specs=[pl.BlockSpec(memory_space=pl.ANY)] * 4,
        out_specs=(pl.BlockSpec(memory_space=pl.ANY),) * 2,
        scratch_shapes=[
            dma((2,)),
            dma((2, n_ctx, n_head)),
            dma((2, n_ctx)),
            dma((2, n_ctx, n_x)),
            dma((2, n_ctx, n_x)),
        ],
        compiler_params=pltpu.CompilerParams(collective_id=0, has_side_effects=True),
        name="fetch",
    )(lat_mine, idx_mine, lat_own, idx_own)


def nt(a, b):
    return lax.dot_general(a, b, (((1,), (1,)), ((), ())), preferred_element_type=F32)


def forward_kernel(src, *refs):
    lat = refs[:GB]
    idx = refs[GB:2 * GB]
    mq, lse, iq, hw, lim, mass, score, keys, ikeys = refs[2 * GB:]
    q = mass.shape[1]
    for b in range(GB):
        keys[b * BLK:(b + 1) * BLK, :] = lat[b][0]
        ikeys[b * BLK:(b + 1) * BLK, :] = idx[b][0]
    mass[...] = jnp.zeros_like(mass)
    score[...] = jnp.zeros_like(score)

    def main(i, carry):
        s = nt(keys[...], mq[i])
        e = jnp.exp2(s * (ATTN_SCALE * LOG2E) - lse[pl.ds(i, 1), :])
        mass[...] += e[:, :q] + e[:, q:]
        return carry

    lax.fori_loop(0, mq.shape[0], main, 0)

    def side(i, carry):
        v = jnp.maximum(nt(ikeys[...], iq[i]), 0.0) * hw[pl.ds(i, 1), :]
        score[...] += v[:, :q] + v[:, q:]
        return carry

    lax.fori_loop(0, iq.shape[0], side, 0)
    offset = lax.broadcasted_iota(jnp.int32, (BLK, q), 0)
    for b in range(GB):
        rows = slice(b * BLK, (b + 1) * BLK)
        seen = offset <= lim[b:b + 1, :]
        mass[rows, :] = jnp.where(seen, mass[rows, :], 0.0)
        score[rows, :] = jnp.where(seen, score[rows, :], -1e30)


def slot_specs(width):
    return [
        pl.BlockSpec((1, BLK, width), lambda g, s, b=b: (s[g * GB + b], 0, 0)) for b in range(GB)
    ]


def forward(source, lat, idx, mq, lse, iq, hw, lim):
    q = lim.shape[1]
    wl, wi = lat.shape[-1], idx.shape[-1]
    rows = GB * BLK
    whole = lambda a: pl.BlockSpec(a.shape, lambda g, s, n=a.ndim: (0,) * n)
    return pl.pallas_call(
        forward_kernel,
        grid_spec=pltpu.PrefetchScalarGridSpec(
            num_scalar_prefetch=1,
            grid=(UB // GB,),
            in_specs=slot_specs(wl) + slot_specs(wi) + [whole(mq), whole(lse), whole(iq), whole(hw)]
            + [pl.BlockSpec((GB, q), lambda g, s: (g, 0))],
            out_specs=(pl.BlockSpec((rows, q), lambda g, s: (g, 0)),) * 2,
            scratch_shapes=[pltpu.VMEM((rows, wl), BF16), pltpu.VMEM((rows, wi), BF16)],
        ),
        out_shape=(jax.ShapeDtypeStruct((UB * BLK, q), F32),) * 2,
        compiler_params=pltpu.CompilerParams(vmem_limit_bytes=VMEM_LIMIT),
        name="forward",
    )(source, *([lat] * GB), *([idx] * GB), mq, lse, iq, hw, lim)


def grad_kernel(n_head, mass, score, cot, grad, got_a, part, got_b, stat, whole,
                ra, rb, rs, rg, sa, sb, ss, sg):
    head, x, core, partner = place()
    n_x = n_head // 2
    span = mass.shape[0] // n_head
    xs = [lax.rem(x + k, n_x) for k in range(1, n_x)]
    heads = [lax.rem(head + k, n_head) for k in range(1, n_head)]
    greet([{"head": h} for h in heads])
    rows = lambda h: pl.ds(pl.multiple_of(h * span, span), span)
    both = (score, mass)
    pending = []
    order = xs + [x]
    for v in order:
        for a in range(2):
            c = remote(both[a].at[rows(v * 2 + 1 - core)], got_a.at[a, v], sa.at[a, v],
                       ra.at[a, v], {"head": partner})
            c.start()
            pending.append(c)
    for i, v in enumerate(order):
        for a in range(2):
            remote(got_a.at[a, v], got_a.at[a, v], sa.at[a, v], ra.at[a, v],
                   {"head": partner}).wait_recv()
            part[a, v] = both[a][rows(v * 2 + core), :] + got_a[a, v]
            if i < n_x - 1:
                c = remote(part.at[a, v], got_b.at[a, x], sb.at[a, v], rb.at[a, x],
                           {"head": v * 2 + core})
                c.start()
                pending.append(c)
    for v in xs:
        for a in range(2):
            remote(got_b.at[a, v], got_b.at[a, v], sb.at[a, v], rb.at[a, v],
                   {"head": partner}).wait_recv()
            part[a, x] += got_b[a, v]
    top = jnp.max(part[0, x], axis=0, keepdims=True)
    expo = jnp.exp(part[0, x] - top)
    stat[head, 0:1, :] = top
    stat[head, 1:2, :] = jnp.sum(expo, axis=0, keepdims=True)
    stat[head, 2:3, :] = jnp.sum(part[1, x], axis=0, keepdims=True)
    stat[head, 3:8, :] = jnp.zeros((5, top.shape[1]), F32)
    for i, h in enumerate(heads):
        c = remote(stat.at[head], stat.at[head], ss.at[i], rs.at[head], {"head": h})
        c.start()
        pending.append(c)
    for h in heads:
        remote(stat.at[h], stat.at[h], ss.at[0], rs.at[h], {"head": partner}).wait_recv()
    best = stat[0, 0:1, :]
    for h in range(1, n_head):
        best = jnp.maximum(best, stat[h, 0:1, :])
    total = jnp.zeros_like(best)
    mass_total = jnp.zeros_like(best)
    for h in range(n_head):
        total += stat[h, 1:2, :] * jnp.exp(stat[h, 0:1, :] - best)
        mass_total += stat[h, 2:3, :]
    left = cot[...] * jnp.exp(top - best) / total
    right = cot[...] / mass_total
    whole[head] = expo * left - part[1, x] * right

    def send(h, sem, to):
        c = remote(whole.at[h], whole.at[h], sem, rg.at[h], {"head": to})
        c.start()
        pending.append(c)

    def arrived(h):
        remote(whole.at[h], whole.at[h], sg.at[0], rg.at[h], {"head": partner}).wait_recv()

    for i, v in enumerate(xs):
        send(head, sg.at[i], v * 2 + core)
    send(head, sg.at[n_x], partner)
    for i, v in enumerate(xs):
        arrived(v * 2 + core)
        send(v * 2 + core, sg.at[n_x + 1 + i], partner)
    for v in [x] + xs:
        arrived(v * 2 + 1 - core)
    for c in pending:
        c.wait_send()
    for h in range(n_head):
        grad[h * span:(h + 1) * span, :] = whole[h]


def score_grads(n_head, mass, score, cot):
    keys, q = mass.shape
    n_x, span = n_head // 2, keys // n_head
    dma = pltpu.SemaphoreType.DMA
    vm = pl.BlockSpec(memory_space=pltpu.VMEM)
    return pl.pallas_call(
        functools.partial(grad_kernel, n_head),
        out_shape=jax.ShapeDtypeStruct((keys, q), F32),
        in_specs=[vm] * 3,
        out_specs=vm,
        scratch_shapes=[
            pltpu.VMEM((2, n_x, span, q), F32),
            pltpu.VMEM((2, n_x, span, q), F32),
            pltpu.VMEM((2, n_x, span, q), F32),
            pltpu.VMEM((n_head, 8, q), F32),
            pltpu.VMEM((n_head, span, q), F32),
            dma((2, n_x)), dma((2, n_x)), dma((n_head,)), dma((n_head,)),
            dma((2, n_x)), dma((2, n_x)), dma((n_head,)), dma((n_head + 1,)),
        ],
        compiler_params=pltpu.CompilerParams(
            collective_id=1, has_side_effects=True, vmem_limit_bytes=VMEM_LIMIT
        ),
        name="score_grads",
    )(mass, score, cot)


def backward_kernel(src, *refs):
    idx = refs[:GB]
    iq, hw, grad, dq, dw, dk, ikeys, tkeys, acc, gacc = refs[GB:]
    q = grad.shape[1]
    step = pl.program_id(0)

    @pl.when(step == 0)
    def _():
        acc[...] = jnp.zeros_like(acc)
        dw[...] = jnp.zeros_like(dw)

    for b in range(GB):
        ikeys[b * BLK:(b + 1) * BLK, :] = idx[b][0]
    tkeys[...] = jnp.swapaxes(ikeys[...].astype(F32), 0, 1).astype(BF16)
    gacc[...] = jnp.zeros_like(gacc)

    def one(i, carry):
        pre = nt(ikeys[...], iq[i])
        g = jnp.concatenate([grad[...], grad[...]], axis=1)
        dw[pl.ds(i, 1), :] += jnp.sum(g * jnp.maximum(pre, 0.0), axis=0, keepdims=True)
        pg = jnp.where(pre > 0.0, g * hw[pl.ds(i, 1), :], 0.0).astype(BF16)
        acc[i] += jnp.dot(tkeys[...], pg, preferred_element_type=F32)
        gacc[...] += jnp.dot(pg, iq[i], preferred_element_type=F32)
        return carry

    lax.fori_loop(0, iq.shape[0], one, 0)
    dk[...] = gacc[...]

    @pl.when(step == pl.num_programs(0) - 1)
    def _():
        for i in range(iq.shape[0]):
            dq[i] = jnp.swapaxes(acc[i], 0, 1).astype(BF16)


def backward(source, idx, iq, hw, grad):
    q = grad.shape[1]
    wi = idx.shape[-1]
    rows = GB * BLK
    pairs = iq.shape[0]
    whole = lambda a: pl.BlockSpec(a.shape, lambda g, s, n=a.ndim: (0,) * n)
    return pl.pallas_call(
        backward_kernel,
        grid_spec=pltpu.PrefetchScalarGridSpec(
            num_scalar_prefetch=1,
            grid=(UB // GB,),
            in_specs=slot_specs(wi) + [whole(iq), whole(hw), pl.BlockSpec((rows, q), lambda g, s: (g, 0))],
            out_specs=(
                pl.BlockSpec((pairs, 2 * q, wi), lambda g, s: (0, 0, 0)),
                pl.BlockSpec((pairs, 2 * q), lambda g, s: (0, 0)),
                pl.BlockSpec((rows, wi), lambda g, s: (g, 0)),
            ),
            scratch_shapes=[
                pltpu.VMEM((rows, wi), BF16),
                pltpu.VMEM((wi, rows), BF16),
                pltpu.VMEM((pairs, wi, 2 * q), F32),
                pltpu.VMEM((rows, wi), F32),
            ],
        ),
        out_shape=(
            jax.ShapeDtypeStruct((pairs, 2 * q, wi), BF16),
            jax.ShapeDtypeStruct((pairs, 2 * q), F32),
            jax.ShapeDtypeStruct((UB * BLK, wi), F32),
        ),
        compiler_params=pltpu.CompilerParams(vmem_limit_bytes=VMEM_LIMIT),
        name="backward",
    )(source, *([idx] * GB), iq, hw, grad)


def return_kernel(n_ctx, n_head, pick, dk, out, got_a, part, got_b, slots, landed,
                  ra, rb, rc, sa, sb, sc, sx, sp, so):
    me = lax.axis_index("ctx")
    head, x, core, partner = place()
    n_x = n_head // 2
    per = slots.shape[1]
    others = [lax.rem(me + k, n_ctx) for k in range(1, n_ctx)]
    xs = [lax.rem(x + k, n_x) for k in range(1, n_x)]
    greet([{"ctx": o} for o in others] + [{"head": v * 2 + core} for v in xs] + [{"head": partner}])
    pending = []
    order = xs + [x]
    for v in order:
        c = remote(dk.at[v * 2 + 1 - core], got_a.at[v], sa.at[v], ra.at[v], {"head": partner})
        c.start()
        pending.append(c)
    for i, v in enumerate(order):
        remote(got_a.at[v], got_a.at[v], sa.at[v], ra.at[v], {"head": partner}).wait_recv()
        part[v] = dk[v * 2 + core] + got_a[v]
        if i < n_x - 1:
            c = remote(part.at[v], got_b.at[x], sb.at[v], rb.at[x], {"head": v * 2 + core})
            c.start()
            pending.append(c)
    for v in xs:
        remote(got_b.at[v], got_b.at[v], sb.at[v], rb.at[v], {"head": partner}).wait_recv()
        part[x] += got_b[v]

    for i, o in enumerate(others + [me]):
        def fill(k, carry, o=o):
            slots[o, k] = part[x, pick[o, k]]
            return carry

        lax.fori_loop(0, per, fill, 0)
        if i < n_ctx - 1:
            c = remote(slots.at[o], landed.at[me, head], sc.at[i], rc.at[me, head], {"ctx": o})
            c.start()
            pending.append(c)
    landed[me, head] = slots[me]

    def arrived(o, h):
        remote(landed.at[o, h], landed.at[o, h], sc.at[0], rc.at[o, h], {"head": partner}).wait_recv()

    def send(o, h, sem, to):
        c = remote(landed.at[o, h], landed.at[o, h], sem, rc.at[o, h], {"head": to})
        c.start()
        pending.append(c)

    sources = [me] + [lax.rem(me + n_ctx - k, n_ctx) for k in range(1, n_ctx)]
    for i, o in enumerate(sources):
        if i > 0:
            arrived(o, head)
        for j, v in enumerate(xs):
            send(o, head, sx.at[i, j], v * 2 + core)
        send(o, head, sp.at[i, 0], partner)
    for i, o in enumerate(sources):
        for j, v in enumerate(xs):
            arrived(o, v * 2 + core)
            send(o, v * 2 + core, sp.at[i, 1 + j], partner)
    for i, o in enumerate(sources):
        for v in [x] + xs:
            arrived(o, v * 2 + 1 - core)
    for c in pending:
        c.wait_send()
    c = pltpu.make_async_copy(landed, out, so)
    c.start()
    c.wait()


def give_back(n_ctx, n_head, pick, dk):
    _, u, _, wi = dk.shape
    n_x = n_head // 2
    per = pick.shape[1]
    dma = pltpu.SemaphoreType.DMA
    vm = pl.BlockSpec(memory_space=pltpu.VMEM)
    return pl.pallas_call(
        functools.partial(return_kernel, n_ctx, n_head),
        out_shape=jax.ShapeDtypeStruct((n_ctx, n_head, per, BLK, wi), F32),
        in_specs=[pl.BlockSpec(memory_space=pltpu.SMEM), vm],
        out_specs=pl.BlockSpec(memory_space=pl.ANY),
        scratch_shapes=[
            pltpu.VMEM((n_x, u, BLK, wi), F32),
            pltpu.VMEM((n_x, u, BLK, wi), F32),
            pltpu.VMEM((n_x, u, BLK, wi), F32),
            pltpu.VMEM((n_ctx, per, BLK, wi), F32),
            pltpu.VMEM((n_ctx, n_head, per, BLK, wi), F32),
            dma((n_x,)), dma((n_x,)), dma((n_ctx, n_head)),
            dma((n_x,)), dma((n_x,)), dma((n_ctx,)), dma((n_ctx, n_x)), dma((n_ctx, n_x)),
            dma(()),
        ],
        compiler_params=pltpu.CompilerParams(
            collective_id=2, has_side_effects=True, vmem_limit_bytes=VMEM_LIMIT
        ),
        name="give_back",
    )(pick, dk)


def land_kernel(asked, got, out):
    out[...] = jnp.zeros_like(out)

    def one(f, carry):
        @pl.when(asked[f] >= 0)
        def _():
            out[asked[f]] += got[f]

        return carry

    lax.fori_loop(0, got.shape[0], one, 0)


def land(asked, got, blocks):
    return pl.pallas_call(
        land_kernel,
        out_shape=jax.ShapeDtypeStruct((blocks,) + got.shape[1:], F32),
        in_specs=[pl.BlockSpec(memory_space=pltpu.SMEM), pl.BlockSpec(memory_space=pltpu.VMEM)],
        out_specs=pl.BlockSpec(memory_space=pltpu.VMEM),
        compiler_params=pltpu.CompilerParams(vmem_limit_bytes=VMEM_LIMIT),
        name="land",
    )(asked, got)


def body(
    main_queries,
    latent_keys,
    lse,
    index_queries,
    index_keys,
    head_weights,
    loss_cotangent,
    block_ids,
):
    n_ctx = lax.axis_size("ctx")
    n_head = lax.axis_size("head")
    me = lax.axis_index("ctx")
    head = lax.axis_index("head")
    q, hm, wl = main_queries.shape
    key_rows, wi = index_keys.shape
    ih = index_queries.shape[1]
    owner_blocks = key_rows // BLK
    per = 2 * UB // n_ctx // n_head
    per_head = UB // n_head
    all_blocks = owner_blocks * n_ctx
    n_slot = n_ctx * n_head * per
    blocks = jnp.arange(all_blocks, dtype=jnp.int32)
    present = jnp.any(block_ids.reshape(-1)[:, None] == blocks[None, :], axis=0)
    grid = present.astype(jnp.int32).reshape(n_ctx, owner_blocks)
    count = jnp.sum(grid, axis=1)
    first = jnp.cumsum(count) - count
    inner = jnp.cumsum(grid, axis=1) - 1
    union = (first[:, None] + inner).reshape(-1)
    inner = inner.reshape(-1)
    owner, local = blocks // owner_blocks, blocks % owner_blocks
    klass, turn = union % n_head, inner // n_head
    slot = (owner * n_head + klass) * per + turn
    spot = klass * per_head + union // n_head
    slot_iota = jnp.arange(n_slot, dtype=jnp.int32)
    union_iota = jnp.arange(UB, dtype=jnp.int32)
    in_slot = present[:, None] & (slot[:, None] == slot_iota[None, :])
    in_union = present[:, None] & (spot[:, None] == union_iota[None, :])
    wanted = jnp.max(jnp.where(in_slot, local[:, None], -1), axis=0)
    pick = jnp.max(jnp.where(in_slot, (union // n_head)[:, None], 0), axis=0)
    source = jnp.max(jnp.where(in_union, slot[:, None], 0), axis=0)
    union_block = jnp.max(jnp.where(in_union, blocks[:, None], 0), axis=0)
    asked = lax.all_to_all(
        wanted.reshape(n_ctx, n_head * per), "ctx", split_axis=0, concat_axis=0, tiled=True
    )
    lat_local = latent_keys.reshape(owner_blocks, BLK, wl)
    idx_local = index_keys.reshape(owner_blocks, BLK, wi)
    want3 = wanted.reshape(n_ctx, n_head, per)
    ask3 = asked.reshape(n_ctx, n_head, per)
    mine = jnp.maximum(lax.dynamic_index_in_dim(ask3, head, 1, keepdims=False), 0)
    own = jnp.maximum(lax.dynamic_index_in_dim(want3, me, 0, keepdims=False), 0)
    my_pick = lax.dynamic_index_in_dim(pick.reshape(n_ctx, n_head, per), head, 1, keepdims=False)
    lat_got, idx_got = fetch(
        n_ctx, n_head, lat_local[mine], idx_local[mine], lat_local[own], idx_local[own]
    )
    lat_got = lat_got.reshape(n_slot, BLK, wl)
    idx_got = idx_got.reshape(n_slot, BLK, wi)
    chosen = jnp.any(union_block[:, None, None] == block_ids[None, :, :], axis=2)
    query_pos = all_blocks * BLK - q * n_ctx + me * q + jnp.arange(q, dtype=jnp.int32)
    lim = jnp.where(chosen, query_pos[None, :] - union_block[:, None] * BLK, -1)
    mq = main_queries.transpose(1, 0, 2).reshape(hm // 2, 2 * q, wl)
    iq = index_queries.transpose(1, 0, 2).reshape(ih // 2, 2 * q, wi)
    lse2 = (lse * LOG2E).T.reshape(hm // 2, 2 * q)
    hw2 = head_weights.T.reshape(ih // 2, 2 * q)
    mass, score = forward(source, lat_got, idx_got, mq, lse2, iq, hw2, lim)
    grad = score_grads(n_head, mass, score, loss_cotangent.reshape(1, q))
    dq, dw, dk = backward(source, idx_got, iq, hw2, grad)
    d_queries = dq.reshape(ih, q, wi).transpose(1, 0, 2)
    d_weights = dw.reshape(ih, q).T
    back = give_back(n_ctx, n_head, my_pick, dk.reshape(n_head, per_head, BLK, wi))
    d_keys = land(asked.reshape(-1), back.reshape(n_slot, BLK, wi), owner_blocks)
    return (d_queries, d_weights, d_keys.reshape(key_rows, wi))


def solution(mesh):
    placed = (
        P(("grp", "ctx"), "head", None),
        P(("grp", "ctx"), None),
        P(("grp", "ctx"), "head"),
        P(("grp", "ctx"), "head", None),
        P(("grp", "ctx"), None),
        P(("grp", "ctx"), "head"),
        P(("grp", "ctx")),
        P(("grp", "ctx"), None),
    )
    return jax.shard_map(
        body,
        mesh=mesh,
        in_specs=placed,
        out_specs=(
            P(("grp", "ctx"), "head", None),
            P(("grp", "ctx"), "head"),
            P(("grp", "ctx"), None),
        ),
        check_vma=False,
    )
```

```python
import functools
import math

import jax
import jax.numpy as jnp
from jax import lax
from jax.experimental import pallas as pl
from jax.experimental.pallas import tpu as pltpu
from jax.sharding import PartitionSpec as P

BLK = 64
UB = 64
GB = 8
ATTN_SCALE = 192.0 ** (-0.5)
LOG2E = math.log2(math.e)
MESH = pl.DeviceIdType.MESH
VMEM_LIMIT = 56 * 1024 * 1024
F32 = jnp.float32
BF16 = jnp.bfloat16


def place():
    head = lax.axis_index("head")
    x, core = head // 2, lax.rem(head, 2)
    return head, x, core, x * 2 + 1 - core


def greet(peers):
    barrier = pltpu.get_barrier_semaphore()
    for peer in peers:
        pl.semaphore_signal(barrier, inc=1, device_id=peer, device_id_type=MESH)
    pl.semaphore_wait(barrier, len(peers))


def remote(src, dst, send, recv, peer):
    return pltpu.make_async_remote_copy(
        src_ref=src, dst_ref=dst, send_sem=send, recv_sem=recv,
        device_id=peer, device_id_type=MESH,
    )


def fetch_kernel(n_ctx, n_head, cuts, lat_mine, idx_mine, lat_own, idx_own, lat_got, idx_got,
                 own_sem, recv_sem, s_ctx, s_x, s_core):
    me = lax.axis_index("ctx")
    head, x, core, partner = place()
    n_x = n_head // 2
    piece = lat_mine.shape[1] // cuts
    others = [lax.rem(me + k, n_ctx) for k in range(1, n_ctx)]
    sources = [lax.rem(me + n_ctx - k, n_ctx) for k in range(1, n_ctx)]
    xs = [lax.rem(x + k, n_x) for k in range(1, n_x)]
    greet([{"ctx": o} for o in others] + [{"head": v * 2 + core} for v in xs] + [{"head": partner}])
    units = range(cuts + 1)

    def mine(a, o):
        return idx_mine.at[o] if a == 0 else lat_mine.at[o, pl.ds((a - 1) * piece, piece)]

    def got(a, o, h):
        return idx_got.at[o, h] if a == 0 else lat_got.at[o, h, pl.ds((a - 1) * piece, piece)]

    pending = []
    for a in units:
        for i, o in enumerate(others):
            c = remote(mine(a, o), got(a, me, head), s_ctx.at[a, i],
                       recv_sem.at[a, me, head], {"ctx": o})
            c.start()
            pending.append(c)
    locals_ = [
        pltpu.make_async_copy(idx_own, idx_got.at[me], own_sem.at[0]),
        pltpu.make_async_copy(lat_own, lat_got.at[me], own_sem.at[1]),
    ]
    for c in locals_:
        c.start()

    def arrived(a, o, h):
        remote(got(a, o, h), got(a, o, h), s_core.at[a, 0, 0], recv_sem.at[a, o, h],
               {"head": partner}).wait_recv()

    def send(a, o, h, sem, to):
        c = remote(got(a, o, h), got(a, o, h), sem, recv_sem.at[a, o, h], {"head": to})
        c.start()
        pending.append(c)

    def across(a):
        for i, o in enumerate(sources):
            arrived(a, o, head)
            for j, v in enumerate(xs):
                send(a, o, head, s_x.at[a, i, j], v * 2 + core)
            send(a, o, head, s_core.at[a, i, 0], partner)

    def along(a):
        for i, o in enumerate(sources):
            for j, v in enumerate(xs):
                arrived(a, o, v * 2 + core)
                send(a, o, v * 2 + core, s_core.at[a, i, 1 + j], partner)

    for a in units:
        across(a)
        if a > 0:
            along(a - 1)
    along(cuts)
    for a in units:
        for i, o in enumerate(sources):
            for v in [x] + xs:
                arrived(a, o, v * 2 + 1 - core)
    for c in pending:
        c.wait_send()
    for c in locals_:
        c.wait()


def fetch(n_ctx, n_head, lat_mine, idx_mine, lat_own, idx_own):
    per, _, wl = lat_mine.shape[1:]
    wi = idx_mine.shape[-1]
    n_x = n_head // 2
    cuts = math.gcd(per, 4)
    dma = pltpu.SemaphoreType.DMA
    return pl.pallas_call(
        functools.partial(fetch_kernel, n_ctx, n_head, cuts),
        out_shape=(
            jax.ShapeDtypeStruct((n_ctx, n_head, per, BLK, wl), BF16),
            jax.ShapeDtypeStruct((n_ctx, n_head, per, BLK, wi), BF16),
        ),
        in_specs=[pl.BlockSpec(memory_space=pl.ANY)] * 4,
        out_specs=(pl.BlockSpec(memory_space=pl.ANY),) * 2,
        scratch_shapes=[
            dma((2,)),
            dma((cuts + 1, n_ctx, n_head)),
            dma((cuts + 1, n_ctx)),
            dma((cuts + 1, n_ctx, n_x)),
            dma((cuts + 1, n_ctx, n_x)),
        ],
        compiler_params=pltpu.CompilerParams(collective_id=0, has_side_effects=True),
        name="fetch",
    )(lat_mine, idx_mine, lat_own, idx_own)


def select_kernel(mine, own, lat, idx, lat_mine, idx_mine, lat_own, idx_own, sem):
    def one(k, carry):
        pltpu.make_async_copy(lat.at[mine[k]], lat_mine.at[k], sem.at[0]).start()
        pltpu.make_async_copy(idx.at[mine[k]], idx_mine.at[k], sem.at[1]).start()
        return carry

    def two(k, carry):
        pltpu.make_async_copy(lat.at[own[k]], lat_own.at[k], sem.at[2]).start()
        pltpu.make_async_copy(idx.at[own[k]], idx_own.at[k], sem.at[3]).start()
        return carry

    lax.fori_loop(0, mine.shape[0], one, 0)
    lax.fori_loop(0, own.shape[0], two, 0)
    for i, r in enumerate((lat_mine, idx_mine, lat_own, idx_own)):
        pltpu.make_async_copy(r, r, sem.at[i]).wait()


def select(mine, own, lat, idx):
    shapes = tuple(
        jax.ShapeDtypeStruct((n,) + a.shape[1:], BF16)
        for n in (mine.shape[0], own.shape[0]) for a in (lat, idx)
    )
    anywhere = pl.BlockSpec(memory_space=pl.ANY)
    return pl.pallas_call(
        select_kernel,
        out_shape=shapes,
        in_specs=[pl.BlockSpec(memory_space=pltpu.SMEM)] * 2 + [anywhere] * 2,
        out_specs=(anywhere,) * 4,
        scratch_shapes=[pltpu.SemaphoreType.DMA((4,))],
        name="select",
    )(mine, own, lat, idx)


def forward_kernel(src, *refs):
    lat = refs[:GB]
    idx = refs[GB:2 * GB]
    mq, lse, iq, hw, lim, mass, score, keys, ikeys = refs[2 * GB:]
    q = mass.shape[1]
    for b in range(GB):
        keys[b * BLK:(b + 1) * BLK, :] = lat[b][0]
        ikeys[b * BLK:(b + 1) * BLK, :] = idx[b][0]
    mass[...] = jnp.zeros_like(mass)
    score[...] = jnp.zeros_like(score)

    def main(i, carry):
        both = jnp.concatenate([mq[2 * i], mq[2 * i + 1]], axis=1)
        s = jnp.dot(keys[...], both, preferred_element_type=F32)
        e = jnp.exp2(s * (ATTN_SCALE * LOG2E) - lse[pl.ds(i, 1), :])
        mass[...] += e[:, :q] + e[:, q:]
        return carry

    lax.fori_loop(0, mq.shape[0] // 2, main, 0, unroll=True)

    def side(i, carry):
        v = jnp.maximum(jnp.dot(ikeys[...], iq[i], preferred_element_type=F32), 0.0) * hw[pl.ds(i, 1), :]
        score[...] += v[:, :q] + v[:, q:]
        return carry

    lax.fori_loop(0, iq.shape[0], side, 0, unroll=True)
    offset = lax.broadcasted_iota(jnp.int32, (BLK, q), 0)
    for b in range(GB):
        rows = slice(b * BLK, (b + 1) * BLK)
        seen = offset <= lim[b:b + 1, :]
        mass[rows, :] = jnp.where(seen, mass[rows, :], 0.0)
        score[rows, :] = jnp.where(seen, score[rows, :], -1e30)


def slot_specs(width):
    return [
        pl.BlockSpec((1, BLK, width), lambda g, s, b=b: (s[g * GB + b], 0, 0)) for b in range(GB)
    ]


def forward(source, lat, idx, mq, lse, iq, hw, lim):
    q = lim.shape[1]
    wl, wi = lat.shape[-1], idx.shape[-1]
    rows = GB * BLK
    whole = lambda a: pl.BlockSpec(a.shape, lambda g, s, n=a.ndim: (0,) * n)
    return pl.pallas_call(
        forward_kernel,
        grid_spec=pltpu.PrefetchScalarGridSpec(
            num_scalar_prefetch=1,
            grid=(UB // GB,),
            in_specs=slot_specs(wl) + slot_specs(wi) + [whole(mq), whole(lse), whole(iq), whole(hw)]
            + [pl.BlockSpec((GB, q), lambda g, s: (g, 0))],
            out_specs=(pl.BlockSpec((rows, q), lambda g, s: (g, 0)),) * 2,
            scratch_shapes=[pltpu.VMEM((rows, wl), BF16), pltpu.VMEM((rows, wi), BF16)],
        ),
        out_shape=(jax.ShapeDtypeStruct((UB * BLK, q), F32),) * 2,
        compiler_params=pltpu.CompilerParams(vmem_limit_bytes=VMEM_LIMIT),
        name="forward",
    )(source, *([lat] * GB), *([idx] * GB), mq, lse, iq, hw, lim)


def grad_kernel(n_head, mass, score, cot, grad, got_a, part, half, got_s, got_m, stat, whole,
                ra, rb, rs, rg, sa, sb, ss, sg):
    head, x, core, partner = place()
    n_x = n_head // 2
    span = mass.shape[0] // n_head
    xs = [lax.rem(x + k, n_x) for k in range(1, n_x)]
    heads = [lax.rem(head + k, n_head) for k in range(1, n_head)]
    greet([{"head": h} for h in heads])
    rows = lambda h: pl.ds(pl.multiple_of(h * span, span), span)
    both = (score, mass)
    got_b = (got_s, got_m)
    pending = []
    order = xs + [x]
    for v in order:
        for a in range(2):
            c = remote(both[a].at[rows(v * 2 + 1 - core)], got_a.at[a, v], sa.at[a, v],
                       ra.at[a, v], {"head": partner})
            c.start()
            pending.append(c)
    for i, v in enumerate(order):
        for a in range(2):
            remote(got_a.at[a, v], got_a.at[a, v], sa.at[a, v], ra.at[a, v],
                   {"head": partner}).wait_recv()
            part[a, v] = both[a][rows(v * 2 + core), :] + got_a[a, v]
            if i < n_x - 1:
                if a == 1:
                    half[v] = part[1, v].astype(BF16)
                c = remote((part.at[0, v] if a == 0 else half.at[v]), got_b[a].at[x], sb.at[a, v], rb.at[a, x],
                           {"head": v * 2 + core})
                c.start()
                pending.append(c)
    for v in xs:
        for a in range(2):
            remote(got_b[a].at[v], got_b[a].at[v], sb.at[a, v], rb.at[a, v],
                   {"head": partner}).wait_recv()
            part[a, x] += got_b[a][v].astype(F32)
    top = jnp.max(part[0, x], axis=0, keepdims=True)
    expo = jnp.exp(part[0, x] - top)
    stat[head, 0:1, :] = top
    stat[head, 1:2, :] = jnp.sum(expo, axis=0, keepdims=True)
    stat[head, 2:3, :] = jnp.sum(part[1, x], axis=0, keepdims=True)
    stat[head, 3:8, :] = jnp.zeros((5, top.shape[1]), F32)
    for i, h in enumerate(heads):
        c = remote(stat.at[head], stat.at[head], ss.at[i], rs.at[head], {"head": h})
        c.start()
        pending.append(c)
    for h in heads:
        remote(stat.at[h], stat.at[h], ss.at[0], rs.at[h], {"head": partner}).wait_recv()
    best = stat[0, 0:1, :]
    for h in range(1, n_head):
        best = jnp.maximum(best, stat[h, 0:1, :])
    total = jnp.zeros_like(best)
    mass_total = jnp.zeros_like(best)
    for h in range(n_head):
        total += stat[h, 1:2, :] * jnp.exp(stat[h, 0:1, :] - best)
        mass_total += stat[h, 2:3, :]
    left = cot[...] * jnp.exp(top - best) / total
    right = cot[...] / mass_total
    whole[head] = (expo * left - part[1, x] * right).astype(BF16)

    def send(h, sem, to):
        c = remote(whole.at[h], whole.at[h], sem, rg.at[h], {"head": to})
        c.start()
        pending.append(c)

    def arrived(h):
        remote(whole.at[h], whole.at[h], sg.at[0], rg.at[h], {"head": partner}).wait_recv()

    for i, v in enumerate(xs):
        send(head, sg.at[i], v * 2 + core)
    send(head, sg.at[n_x], partner)
    for i, v in enumerate(xs):
        arrived(v * 2 + core)
        send(v * 2 + core, sg.at[n_x + 1 + i], partner)
    for v in [x] + xs:
        arrived(v * 2 + 1 - core)
    for c in pending:
        c.wait_send()
    for h in range(n_head):
        grad[h * span:(h + 1) * span, :] = whole[h]


def score_grads(n_head, mass, score, cot):
    keys, q = mass.shape
    n_x, span = n_head // 2, keys // n_head
    dma = pltpu.SemaphoreType.DMA
    vm = pl.BlockSpec(memory_space=pltpu.VMEM)
    return pl.pallas_call(
        functools.partial(grad_kernel, n_head),
        out_shape=jax.ShapeDtypeStruct((keys, q), BF16),
        in_specs=[vm] * 3,
        out_specs=vm,
        scratch_shapes=[
            pltpu.VMEM((2, n_x, span, q), F32),
            pltpu.VMEM((2, n_x, span, q), F32),
            pltpu.VMEM((n_x, span, q), BF16),
            pltpu.VMEM((n_x, span, q), F32),
            pltpu.VMEM((n_x, span, q), BF16),
            pltpu.VMEM((n_head, 8, q), F32),
            pltpu.VMEM((n_head, span, q), BF16),
            dma((2, n_x)), dma((2, n_x)), dma((n_head,)), dma((n_head,)),
            dma((2, n_x)), dma((2, n_x)), dma((n_head,)), dma((n_head + 1,)),
        ],
        compiler_params=pltpu.CompilerParams(
            collective_id=1, has_side_effects=True, vmem_limit_bytes=VMEM_LIMIT
        ),
        name="score_grads",
    )(mass, score, cot)


def backward_kernel(src, *refs):
    idx = refs[:GB]
    iq, iqt, hw, grad, dq, dw, dk, ikeys, tkeys, acc, gacc = refs[GB:]
    q = grad.shape[1]
    step = pl.program_id(0)

    @pl.when(step == 0)
    def _():
        acc[...] = jnp.zeros_like(acc)
        dw[...] = jnp.zeros_like(dw)

    for b in range(GB):
        ikeys[b * BLK:(b + 1) * BLK, :] = idx[b][0]
    tkeys[...] = jnp.swapaxes(ikeys[...].astype(F32), 0, 1).astype(BF16)
    gacc[...] = jnp.zeros_like(gacc)

    def one(i, carry):
        pre = jnp.dot(ikeys[...], iqt[i], preferred_element_type=F32)
        half = grad[...].astype(F32)
        g = jnp.concatenate([half, half], axis=1)
        dw[pl.ds(i, 1), :] += jnp.sum(g * jnp.maximum(pre, 0.0), axis=0, keepdims=True)
        pg = jnp.where(pre > 0.0, g * hw[pl.ds(i, 1), :], 0.0).astype(BF16)
        acc[i] += jnp.dot(tkeys[...], pg, preferred_element_type=F32)
        gacc[...] += jnp.dot(pg, iq[i], preferred_element_type=F32)
        return carry

    lax.fori_loop(0, iq.shape[0], one, 0, unroll=True)
    dk[...] = gacc[...]

    @pl.when(step == pl.num_programs(0) - 1)
    def _():
        for i in range(iq.shape[0]):
            dq[i] = jnp.swapaxes(acc[i], 0, 1).astype(BF16)


def backward(source, idx, iq, iqt, hw, grad):
    q = grad.shape[1]
    wi = idx.shape[-1]
    rows = GB * BLK
    pairs = iq.shape[0]
    whole = lambda a: pl.BlockSpec(a.shape, lambda g, s, n=a.ndim: (0,) * n)
    return pl.pallas_call(
        backward_kernel,
        grid_spec=pltpu.PrefetchScalarGridSpec(
            num_scalar_prefetch=1,
            grid=(UB // GB,),
            in_specs=slot_specs(wi) + [whole(iq), whole(iqt), whole(hw), pl.BlockSpec((rows, q), lambda g, s: (g, 0))],
            out_specs=(
                pl.BlockSpec((pairs, 2 * q, wi), lambda g, s: (0, 0, 0)),
                pl.BlockSpec((pairs, 2 * q), lambda g, s: (0, 0)),
                pl.BlockSpec((rows, wi), lambda g, s: (g, 0)),
            ),
            scratch_shapes=[
                pltpu.VMEM((rows, wi), BF16),
                pltpu.VMEM((wi, rows), BF16),
                pltpu.VMEM((pairs, wi, 2 * q), F32),
                pltpu.VMEM((rows, wi), F32),
            ],
        ),
        out_shape=(
            jax.ShapeDtypeStruct((pairs, 2 * q, wi), BF16),
            jax.ShapeDtypeStruct((pairs, 2 * q), F32),
            jax.ShapeDtypeStruct((UB * BLK, wi), F32),
        ),
        compiler_params=pltpu.CompilerParams(vmem_limit_bytes=VMEM_LIMIT),
        name="backward",
    )(source, *([idx] * GB), iq, iqt, hw, grad)


def return_kernel(n_ctx, n_head, pick, dk, out, got_a, part, half, got_b, slots, landed,
                  ra, rb, rc, sa, sb, sc, sx, sp, so):
    me = lax.axis_index("ctx")
    head, x, core, partner = place()
    n_x = n_head // 2
    per = slots.shape[1]
    others = [lax.rem(me + k, n_ctx) for k in range(1, n_ctx)]
    xs = [lax.rem(x + k, n_x) for k in range(1, n_x)]
    greet([{"ctx": o} for o in others] + [{"head": v * 2 + core} for v in xs] + [{"head": partner}])
    pending = []
    order = xs + [x]
    for v in order:
        c = remote(dk.at[v * 2 + 1 - core], got_a.at[v], sa.at[v], ra.at[v], {"head": partner})
        c.start()
        pending.append(c)
    for i, v in enumerate(order):
        remote(got_a.at[v], got_a.at[v], sa.at[v], ra.at[v], {"head": partner}).wait_recv()
        part[v] = dk[v * 2 + core] + got_a[v]
        if i < n_x - 1:
            half[v] = part[v].astype(BF16)
            c = remote(half.at[v], got_b.at[x], sb.at[v], rb.at[x], {"head": v * 2 + core})
            c.start()
            pending.append(c)
    for v in xs:
        remote(got_b.at[v], got_b.at[v], sb.at[v], rb.at[v], {"head": partner}).wait_recv()
        part[x] += got_b[v].astype(F32)

    for i, o in enumerate(others + [me]):
        def fill(k, carry, o=o):
            slots[o, k] = part[x, pick[o, k]].astype(BF16)
            return carry

        lax.fori_loop(0, per, fill, 0)
        if i < n_ctx - 1:
            c = remote(slots.at[o], landed.at[me, head], sc.at[i], rc.at[me, head], {"ctx": o})
            c.start()
            pending.append(c)
    landed[me, head] = slots[me]

    def arrived(o, h):
        remote(landed.at[o, h], landed.at[o, h], sc.at[0], rc.at[o, h], {"head": partner}).wait_recv()

    def send(o, h, sem, to):
        c = remote(landed.at[o, h], landed.at[o, h], sem, rc.at[o, h], {"head": to})
        c.start()
        pending.append(c)

    sources = [me] + [lax.rem(me + n_ctx - k, n_ctx) for k in range(1, n_ctx)]
    for i, o in enumerate(sources):
        if i > 0:
            arrived(o, head)
        for j, v in enumerate(xs):
            send(o, head, sx.at[i, j], v * 2 + core)
        send(o, head, sp.at[i, 0], partner)
    for i, o in enumerate(sources):
        for j, v in enumerate(xs):
            arrived(o, v * 2 + core)
            send(o, v * 2 + core, sp.at[i, 1 + j], partner)
    for i, o in enumerate(sources):
        for v in [x] + xs:
            arrived(o, v * 2 + 1 - core)
    for c in pending:
        c.wait_send()
    c = pltpu.make_async_copy(landed, out, so)
    c.start()
    c.wait()


def give_back(n_ctx, n_head, pick, dk):
    _, u, _, wi = dk.shape
    n_x = n_head // 2
    per = pick.shape[1]
    dma = pltpu.SemaphoreType.DMA
    vm = pl.BlockSpec(memory_space=pltpu.VMEM)
    return pl.pallas_call(
        functools.partial(return_kernel, n_ctx, n_head),
        out_shape=jax.ShapeDtypeStruct((n_ctx, n_head, per, BLK, wi), BF16),
        in_specs=[pl.BlockSpec(memory_space=pltpu.SMEM), vm],
        out_specs=pl.BlockSpec(memory_space=pl.ANY),
        scratch_shapes=[
            pltpu.VMEM((n_x, u, BLK, wi), F32),
            pltpu.VMEM((n_x, u, BLK, wi), F32),
            pltpu.VMEM((n_x, u, BLK, wi), BF16),
            pltpu.VMEM((n_x, u, BLK, wi), BF16),
            pltpu.VMEM((n_ctx, per, BLK, wi), BF16),
            pltpu.VMEM((n_ctx, n_head, per, BLK, wi), BF16),
            dma((n_x,)), dma((n_x,)), dma((n_ctx, n_head)),
            dma((n_x,)), dma((n_x,)), dma((n_ctx,)), dma((n_ctx, n_x)), dma((n_ctx, n_x)),
            dma(()),
        ],
        compiler_params=pltpu.CompilerParams(
            collective_id=2, has_side_effects=True, vmem_limit_bytes=VMEM_LIMIT
        ),
        name="give_back",
    )(pick, dk)


def land_kernel(asked, got, out):
    out[...] = jnp.zeros_like(out)

    def one(f, carry):
        @pl.when(asked[f] >= 0)
        def _():
            out[asked[f]] += got[f].astype(F32)

        return carry

    lax.fori_loop(0, got.shape[0], one, 0)


def land(asked, got, blocks):
    return pl.pallas_call(
        land_kernel,
        out_shape=jax.ShapeDtypeStruct((blocks,) + got.shape[1:], F32),
        in_specs=[pl.BlockSpec(memory_space=pltpu.SMEM), pl.BlockSpec(memory_space=pltpu.VMEM)],
        out_specs=pl.BlockSpec(memory_space=pltpu.VMEM),
        compiler_params=pltpu.CompilerParams(vmem_limit_bytes=VMEM_LIMIT),
        name="land",
    )(asked, got)


def body(
    main_queries,
    latent_keys,
    lse,
    index_queries,
    index_keys,
    head_weights,
    loss_cotangent,
    block_ids,
):
    n_ctx = lax.axis_size("ctx")
    n_head = lax.axis_size("head")
    me = lax.axis_index("ctx")
    head = lax.axis_index("head")
    q, hm, wl = main_queries.shape
    key_rows, wi = index_keys.shape
    ih = index_queries.shape[1]
    owner_blocks = key_rows // BLK
    per = 2 * UB // n_ctx // n_head
    per_head = UB // n_head
    all_blocks = owner_blocks * n_ctx
    n_slot = n_ctx * n_head * per
    blocks = jnp.arange(all_blocks, dtype=jnp.int32)
    present = jnp.any(block_ids.reshape(-1)[:, None] == blocks[None, :], axis=0)
    grid = present.astype(jnp.int32).reshape(n_ctx, owner_blocks)
    count = jnp.sum(grid, axis=1)
    first = jnp.cumsum(count) - count
    inner = jnp.cumsum(grid, axis=1) - 1
    union = (first[:, None] + inner).reshape(-1)
    inner = inner.reshape(-1)
    owner, local = blocks // owner_blocks, blocks % owner_blocks
    klass, turn = union % n_head, inner // n_head
    slot = (owner * n_head + klass) * per + turn
    spot = klass * per_head + union // n_head
    slot_iota = jnp.arange(n_slot, dtype=jnp.int32)
    union_iota = jnp.arange(UB, dtype=jnp.int32)
    in_slot = present[:, None] & (slot[:, None] == slot_iota[None, :])
    in_union = present[:, None] & (spot[:, None] == union_iota[None, :])
    wanted = jnp.max(jnp.where(in_slot, local[:, None], -1), axis=0)
    pick = jnp.max(jnp.where(in_slot, (union // n_head)[:, None], 0), axis=0)
    source = jnp.max(jnp.where(in_union, slot[:, None], 0), axis=0)
    union_block = jnp.max(jnp.where(in_union, blocks[:, None], 0), axis=0)
    asked = lax.all_to_all(
        wanted.reshape(n_ctx, n_head * per), "ctx", split_axis=0, concat_axis=0, tiled=True
    )
    lat_local = latent_keys.reshape(owner_blocks, BLK, wl)
    idx_local = index_keys.reshape(owner_blocks, BLK, wi)
    want3 = wanted.reshape(n_ctx, n_head, per)
    ask3 = asked.reshape(n_ctx, n_head, per)
    mine = jnp.maximum(lax.dynamic_index_in_dim(ask3, head, 1, keepdims=False), 0)
    own = jnp.maximum(lax.dynamic_index_in_dim(want3, me, 0, keepdims=False), 0)
    my_pick = lax.dynamic_index_in_dim(pick.reshape(n_ctx, n_head, per), head, 1, keepdims=False)
    lat_mine, idx_mine, lat_own, idx_own = select(
        mine.reshape(-1), own.reshape(-1), lat_local, idx_local
    )
    lat_got, idx_got = fetch(
        n_ctx,
        n_head,
        lat_mine.reshape(n_ctx, per, BLK, wl),
        idx_mine.reshape(n_ctx, per, BLK, wi),
        lat_own.reshape(n_head, per, BLK, wl),
        idx_own.reshape(n_head, per, BLK, wi),
    )
    lat_got = lat_got.reshape(n_slot, BLK, wl)
    idx_got = idx_got.reshape(n_slot, BLK, wi)
    chosen = jnp.any(union_block[:, None, None] == block_ids[None, :, :], axis=2)
    query_pos = all_blocks * BLK - q * n_ctx + me * q + jnp.arange(q, dtype=jnp.int32)
    lim = jnp.where(chosen, query_pos[None, :] - union_block[:, None] * BLK, -1)
    mq = main_queries.transpose(1, 2, 0)
    iq = index_queries.transpose(1, 0, 2).reshape(ih // 2, 2 * q, wi)
    iqt = iq.transpose(0, 2, 1)
    lse2 = (lse * LOG2E).T.reshape(hm // 2, 2 * q)
    hw2 = head_weights.T.reshape(ih // 2, 2 * q)
    mass, score = forward(source, lat_got, idx_got, mq, lse2, iqt, hw2, lim)
    grad = score_grads(n_head, mass, score, loss_cotangent.reshape(1, q))
    dq, dw, dk = backward(source, idx_got, iq, iqt, hw2, grad)
    d_queries = dq.reshape(ih, q, wi).transpose(1, 0, 2)
    d_weights = dw.reshape(ih, q).T
    back = give_back(n_ctx, n_head, my_pick, dk.reshape(n_head, per_head, BLK, wi))
    d_keys = land(asked.reshape(-1), back.reshape(n_slot, BLK, wi), owner_blocks)
    return (d_queries, d_weights, d_keys.reshape(key_rows, wi))


def solution(mesh):
    placed = (
        P(("grp", "ctx"), "head", None),
        P(("grp", "ctx"), None),
        P(("grp", "ctx"), "head"),
        P(("grp", "ctx"), "head", None),
        P(("grp", "ctx"), None),
        P(("grp", "ctx"), "head"),
        P(("grp", "ctx")),
        P(("grp", "ctx"), None),
    )
    return jax.shard_map(
        body,
        mesh=mesh,
        in_specs=placed,
        out_specs=(
            P(("grp", "ctx"), "head", None),
            P(("grp", "ctx"), "head"),
            P(("grp", "ctx"), None),
        ),
        check_vma=False,
    )
```

```python
import functools
import math

import jax
import jax.numpy as jnp
from jax import lax
from jax.experimental import pallas as pl
from jax.experimental.pallas import tpu as pltpu
from jax.sharding import PartitionSpec as P

BLK = 64
UB = 64
GB = 8
ATTN_SCALE = 192.0 ** (-0.5)
LOG2E = math.log2(math.e)
MESH = pl.DeviceIdType.MESH
VMEM_LIMIT = 56 * 1024 * 1024
F32 = jnp.float32
BF16 = jnp.bfloat16


def place():
    head = lax.axis_index("head")
    x, core = head // 2, lax.rem(head, 2)
    return head, x, core, x * 2 + 1 - core


def greet(peers):
    barrier = pltpu.get_barrier_semaphore()
    for peer in peers:
        pl.semaphore_signal(barrier, inc=1, device_id=peer, device_id_type=MESH)
    pl.semaphore_wait(barrier, len(peers))


def remote(src, dst, send, recv, peer):
    return pltpu.make_async_remote_copy(
        src_ref=src, dst_ref=dst, send_sem=send, recv_sem=recv,
        device_id=peer, device_id_type=MESH,
    )


def fetch_kernel(n_ctx, n_head, cuts, lat_mine, idx_mine, lat_own, idx_own, lat_got, idx_got,
                 own_sem, recv_sem, s_ctx, s_x, s_core):
    me = lax.axis_index("ctx")
    head, x, core, partner = place()
    n_x = n_head // 2
    piece = lat_mine.shape[1] // cuts
    others = [lax.rem(me + k, n_ctx) for k in range(1, n_ctx)]
    sources = [lax.rem(me + n_ctx - k, n_ctx) for k in range(1, n_ctx)]
    xs = [lax.rem(x + k, n_x) for k in range(1, n_x)]
    greet([{"ctx": o} for o in others] + [{"head": v * 2 + core} for v in xs] + [{"head": partner}])
    units = range(cuts + 1)

    def mine(a, o):
        return idx_mine.at[o] if a == 0 else lat_mine.at[o, pl.ds((a - 1) * piece, piece)]

    def got(a, o, h):
        return idx_got.at[o, h] if a == 0 else lat_got.at[o, h, pl.ds((a - 1) * piece, piece)]

    pending = []
    for a in units:
        for i, o in enumerate(others):
            c = remote(mine(a, o), got(a, me, head), s_ctx.at[a, i],
                       recv_sem.at[a, me, head], {"ctx": o})
            c.start()
            pending.append(c)
    locals_ = [
        pltpu.make_async_copy(idx_own, idx_got.at[me], own_sem.at[0]),
        pltpu.make_async_copy(lat_own, lat_got.at[me], own_sem.at[1]),
    ]
    for c in locals_:
        c.start()

    def arrived(a, o, h):
        remote(got(a, o, h), got(a, o, h), s_core.at[a, 0, 0], recv_sem.at[a, o, h],
               {"head": partner}).wait_recv()

    def send(a, o, h, sem, to):
        c = remote(got(a, o, h), got(a, o, h), sem, recv_sem.at[a, o, h], {"head": to})
        c.start()
        pending.append(c)

    def across(a):
        for i, o in enumerate(sources):
            arrived(a, o, head)
            for j, v in enumerate(xs):
                send(a, o, head, s_x.at[a, i, j], v * 2 + core)
            send(a, o, head, s_core.at[a, i, 0], partner)

    def along(a):
        for i, o in enumerate(sources):
            for j, v in enumerate(xs):
                arrived(a, o, v * 2 + core)
                send(a, o, v * 2 + core, s_core.at[a, i, 1 + j], partner)

    for a in units:
        across(a)
        if a > 0:
            along(a - 1)
    along(cuts)
    for a in units:
        for i, o in enumerate(sources):
            for v in [x] + xs:
                arrived(a, o, v * 2 + 1 - core)
    for c in pending:
        c.wait_send()
    for c in locals_:
        c.wait()


def fetch(n_ctx, n_head, lat_mine, idx_mine, lat_own, idx_own):
    per, _, wl = lat_mine.shape[1:]
    wi = idx_mine.shape[-1]
    n_x = n_head // 2
    cuts = math.gcd(per, 4)
    dma = pltpu.SemaphoreType.DMA
    return pl.pallas_call(
        functools.partial(fetch_kernel, n_ctx, n_head, cuts),
        out_shape=(
            jax.ShapeDtypeStruct((n_ctx, n_head, per, BLK, wl), BF16),
            jax.ShapeDtypeStruct((n_ctx, n_head, per, BLK, wi), BF16),
        ),
        in_specs=[pl.BlockSpec(memory_space=pl.ANY)] * 2
        + [pl.BlockSpec(memory_space=pltpu.VMEM)] * 2,
        out_specs=(pl.BlockSpec(memory_space=pl.ANY),) * 2,
        scratch_shapes=[
            dma((2,)),
            dma((cuts + 1, n_ctx, n_head)),
            dma((cuts + 1, n_ctx)),
            dma((cuts + 1, n_ctx, n_x)),
            dma((cuts + 1, n_ctx, n_x)),
        ],
        compiler_params=pltpu.CompilerParams(
            collective_id=0, has_side_effects=True, vmem_limit_bytes=VMEM_LIMIT
        ),
        name="fetch",
    )(lat_mine, idx_mine, lat_own, idx_own)


def select_kernel(mine, own, lat, idx, lat_mine, idx_mine, lat_own, idx_own, sem):
    def one(k, carry):
        pltpu.make_async_copy(lat.at[mine[k]], lat_mine.at[k], sem.at[0]).start()
        pltpu.make_async_copy(idx.at[mine[k]], idx_mine.at[k], sem.at[1]).start()
        return carry

    def two(k, carry):
        pltpu.make_async_copy(lat.at[own[k]], lat_own.at[k], sem.at[2]).start()
        pltpu.make_async_copy(idx.at[own[k]], idx_own.at[k], sem.at[3]).start()
        return carry

    lax.fori_loop(0, mine.shape[0], one, 0)
    lax.fori_loop(0, own.shape[0], two, 0)
    for i, r in enumerate((lat_mine, idx_mine, lat_own, idx_own)):
        pltpu.make_async_copy(r, r, sem.at[i]).wait()


def select(mine, own, lat, idx):
    shapes = tuple(
        jax.ShapeDtypeStruct((n,) + a.shape[1:], BF16)
        for n in (mine.shape[0], own.shape[0]) for a in (lat, idx)
    )
    anywhere = pl.BlockSpec(memory_space=pl.ANY)
    return pl.pallas_call(
        select_kernel,
        out_shape=shapes,
        in_specs=[pl.BlockSpec(memory_space=pltpu.SMEM)] * 2 + [anywhere] * 2,
        out_specs=(pl.BlockSpec(memory_space=pltpu.VMEM),) * 4,
        scratch_shapes=[pltpu.SemaphoreType.DMA((4,))],
        compiler_params=pltpu.CompilerParams(vmem_limit_bytes=VMEM_LIMIT),
        name="select",
    )(mine, own, lat, idx)


def forward_kernel(src, *refs):
    lat = refs[:GB]
    idx = refs[GB:2 * GB]
    mq, lse, iq, hw, lim, mass, score, keys, ikeys = refs[2 * GB:]
    q = mass.shape[1]
    for b in range(GB):
        keys[b * BLK:(b + 1) * BLK, :] = lat[b][0]
        ikeys[b * BLK:(b + 1) * BLK, :] = idx[b][0]
    mass[...] = jnp.zeros_like(mass)
    score[...] = jnp.zeros_like(score)

    def main(i, carry):
        both = jnp.concatenate([mq[2 * i], mq[2 * i + 1]], axis=1)
        s = jnp.dot(keys[...], both, preferred_element_type=F32)
        e = jnp.exp2(s * (ATTN_SCALE * LOG2E) - lse[pl.ds(i, 1), :])
        mass[...] += e[:, :q] + e[:, q:]
        return carry

    lax.fori_loop(0, mq.shape[0] // 2, main, 0, unroll=True)

    def side(i, carry):
        v = jnp.maximum(jnp.dot(ikeys[...], iq[i], preferred_element_type=F32), 0.0) * hw[pl.ds(i, 1), :]
        score[...] += v[:, :q] + v[:, q:]
        return carry

    lax.fori_loop(0, iq.shape[0], side, 0, unroll=True)
    offset = lax.broadcasted_iota(jnp.int32, (BLK, q), 0)
    for b in range(GB):
        rows = slice(b * BLK, (b + 1) * BLK)
        seen = offset <= lim[b:b + 1, :]
        mass[rows, :] = jnp.where(seen, mass[rows, :], 0.0)
        score[rows, :] = jnp.where(seen, score[rows, :], -1e30)


def slot_specs(width):
    return [
        pl.BlockSpec((1, BLK, width), lambda g, s, b=b: (s[g * GB + b], 0, 0)) for b in range(GB)
    ]


def forward(source, lat, idx, mq, lse, iq, hw, lim):
    q = lim.shape[1]
    wl, wi = lat.shape[-1], idx.shape[-1]
    rows = GB * BLK
    whole = lambda a: pl.BlockSpec(a.shape, lambda g, s, n=a.ndim: (0,) * n)
    return pl.pallas_call(
        forward_kernel,
        grid_spec=pltpu.PrefetchScalarGridSpec(
            num_scalar_prefetch=1,
            grid=(UB // GB,),
            in_specs=slot_specs(wl) + slot_specs(wi) + [whole(mq), whole(lse), whole(iq), whole(hw)]
            + [pl.BlockSpec((GB, q), lambda g, s: (g, 0))],
            out_specs=(pl.BlockSpec((rows, q), lambda g, s: (g, 0)),) * 2,
            scratch_shapes=[pltpu.VMEM((rows, wl), BF16), pltpu.VMEM((rows, wi), BF16)],
        ),
        out_shape=(jax.ShapeDtypeStruct((UB * BLK, q), F32),) * 2,
        compiler_params=pltpu.CompilerParams(vmem_limit_bytes=VMEM_LIMIT),
        name="forward",
    )(source, *([lat] * GB), *([idx] * GB), mq, lse, iq, hw, lim)


def grad_kernel(n_head, mass, score, cot, grad, got_a, part, half, got_s, got_m, stat, whole,
                ra, rb, rs, rg, sa, sb, ss, sg):
    head, x, core, partner = place()
    n_x = n_head // 2
    span = mass.shape[0] // n_head
    xs = [lax.rem(x + k, n_x) for k in range(1, n_x)]
    heads = [lax.rem(head + k, n_head) for k in range(1, n_head)]
    greet([{"head": h} for h in heads])
    rows = lambda h: pl.ds(pl.multiple_of(h * span, span), span)
    both = (score, mass)
    got_b = (got_s, got_m)
    pending = []
    order = xs + [x]
    for v in order:
        for a in range(2):
            c = remote(both[a].at[rows(v * 2 + 1 - core)], got_a.at[a, v], sa.at[a, v],
                       ra.at[a, v], {"head": partner})
            c.start()
            pending.append(c)
    for i, v in enumerate(order):
        for a in range(2):
            remote(got_a.at[a, v], got_a.at[a, v], sa.at[a, v], ra.at[a, v],
                   {"head": partner}).wait_recv()
            part[a, v] = both[a][rows(v * 2 + core), :] + got_a[a, v]
            if i < n_x - 1:
                if a == 1:
                    half[v] = part[1, v].astype(BF16)
                c = remote((part.at[0, v] if a == 0 else half.at[v]), got_b[a].at[x], sb.at[a, v], rb.at[a, x],
                           {"head": v * 2 + core})
                c.start()
                pending.append(c)
    for v in xs:
        for a in range(2):
            remote(got_b[a].at[v], got_b[a].at[v], sb.at[a, v], rb.at[a, v],
                   {"head": partner}).wait_recv()
            part[a, x] += got_b[a][v].astype(F32)
    top = jnp.max(part[0, x], axis=0, keepdims=True)
    expo = jnp.exp(part[0, x] - top)
    stat[head, 0:1, :] = top
    stat[head, 1:2, :] = jnp.sum(expo, axis=0, keepdims=True)
    stat[head, 2:3, :] = jnp.sum(part[1, x], axis=0, keepdims=True)
    stat[head, 3:8, :] = jnp.zeros((5, top.shape[1]), F32)
    for i, h in enumerate(heads):
        c = remote(stat.at[head], stat.at[head], ss.at[i], rs.at[head], {"head": h})
        c.start()
        pending.append(c)
    for h in heads:
        remote(stat.at[h], stat.at[h], ss.at[0], rs.at[h], {"head": partner}).wait_recv()
    best = stat[0, 0:1, :]
    for h in range(1, n_head):
        best = jnp.maximum(best, stat[h, 0:1, :])
    total = jnp.zeros_like(best)
    mass_total = jnp.zeros_like(best)
    for h in range(n_head):
        total += stat[h, 1:2, :] * jnp.exp(stat[h, 0:1, :] - best)
        mass_total += stat[h, 2:3, :]
    left = cot[...] * jnp.exp(top - best) / total
    right = cot[...] / mass_total
    whole[head] = (expo * left - part[1, x] * right).astype(BF16)

    def send(h, sem, to):
        c = remote(whole.at[h], whole.at[h], sem, rg.at[h], {"head": to})
        c.start()
        pending.append(c)

    def arrived(h):
        remote(whole.at[h], whole.at[h], sg.at[0], rg.at[h], {"head": partner}).wait_recv()

    for i, v in enumerate(xs):
        send(head, sg.at[i], v * 2 + core)
    send(head, sg.at[n_x], partner)
    for i, v in enumerate(xs):
        arrived(v * 2 + core)
        send(v * 2 + core, sg.at[n_x + 1 + i], partner)
    for v in [x] + xs:
        arrived(v * 2 + 1 - core)
    for c in pending:
        c.wait_send()
    for h in range(n_head):
        grad[h * span:(h + 1) * span, :] = whole[h]


def score_grads(n_head, mass, score, cot):
    keys, q = mass.shape
    n_x, span = n_head // 2, keys // n_head
    dma = pltpu.SemaphoreType.DMA
    vm = pl.BlockSpec(memory_space=pltpu.VMEM)
    return pl.pallas_call(
        functools.partial(grad_kernel, n_head),
        out_shape=jax.ShapeDtypeStruct((keys, q), BF16),
        in_specs=[vm] * 3,
        out_specs=vm,
        scratch_shapes=[
            pltpu.VMEM((2, n_x, span, q), F32),
            pltpu.VMEM((2, n_x, span, q), F32),
            pltpu.VMEM((n_x, span, q), BF16),
            pltpu.VMEM((n_x, span, q), F32),
            pltpu.VMEM((n_x, span, q), BF16),
            pltpu.VMEM((n_head, 8, q), F32),
            pltpu.VMEM((n_head, span, q), BF16),
            dma((2, n_x)), dma((2, n_x)), dma((n_head,)), dma((n_head,)),
            dma((2, n_x)), dma((2, n_x)), dma((n_head,)), dma((n_head + 1,)),
        ],
        compiler_params=pltpu.CompilerParams(
            collective_id=1, has_side_effects=True, vmem_limit_bytes=VMEM_LIMIT
        ),
        name="score_grads",
    )(mass, score, cot)


def backward_kernel(src, *refs):
    idx = refs[:GB]
    iq, iqt, hw, grad, dq, dw, dk, ikeys, tkeys, acc, gacc = refs[GB:]
    q = grad.shape[1]
    step = pl.program_id(0)

    @pl.when(step == 0)
    def _():
        acc[...] = jnp.zeros_like(acc)
        dw[...] = jnp.zeros_like(dw)

    for b in range(GB):
        ikeys[b * BLK:(b + 1) * BLK, :] = idx[b][0]
    tkeys[...] = jnp.swapaxes(ikeys[...].astype(F32), 0, 1).astype(BF16)
    gacc[...] = jnp.zeros_like(gacc)

    def one(i, carry):
        pre = jnp.dot(ikeys[...], iqt[i], preferred_element_type=F32)
        half = grad[...].astype(F32)
        g = jnp.concatenate([half, half], axis=1)
        dw[pl.ds(i, 1), :] += jnp.sum(g * jnp.maximum(pre, 0.0), axis=0, keepdims=True)
        pg = jnp.where(pre > 0.0, g * hw[pl.ds(i, 1), :], 0.0).astype(BF16)
        acc[i] += jnp.dot(tkeys[...], pg, preferred_element_type=F32)
        gacc[...] += jnp.dot(pg, iq[i], preferred_element_type=F32)
        return carry

    lax.fori_loop(0, iq.shape[0], one, 0, unroll=True)
    dk[...] = gacc[...]

    @pl.when(step == pl.num_programs(0) - 1)
    def _():
        for i in range(iq.shape[0]):
            dq[i] = jnp.swapaxes(acc[i], 0, 1).astype(BF16)


def backward(source, idx, iq, iqt, hw, grad):
    q = grad.shape[1]
    wi = idx.shape[-1]
    rows = GB * BLK
    pairs = iq.shape[0]
    whole = lambda a: pl.BlockSpec(a.shape, lambda g, s, n=a.ndim: (0,) * n)
    return pl.pallas_call(
        backward_kernel,
        grid_spec=pltpu.PrefetchScalarGridSpec(
            num_scalar_prefetch=1,
            grid=(UB // GB,),
            in_specs=slot_specs(wi) + [whole(iq), whole(iqt), whole(hw), pl.BlockSpec((rows, q), lambda g, s: (g, 0))],
            out_specs=(
                pl.BlockSpec((pairs, 2 * q, wi), lambda g, s: (0, 0, 0)),
                pl.BlockSpec((pairs, 2 * q), lambda g, s: (0, 0)),
                pl.BlockSpec((rows, wi), lambda g, s: (g, 0)),
            ),
            scratch_shapes=[
                pltpu.VMEM((rows, wi), BF16),
                pltpu.VMEM((wi, rows), BF16),
                pltpu.VMEM((pairs, wi, 2 * q), F32),
                pltpu.VMEM((rows, wi), F32),
            ],
        ),
        out_shape=(
            jax.ShapeDtypeStruct((pairs, 2 * q, wi), BF16),
            jax.ShapeDtypeStruct((pairs, 2 * q), F32),
            jax.ShapeDtypeStruct((UB * BLK, wi), F32),
        ),
        compiler_params=pltpu.CompilerParams(vmem_limit_bytes=VMEM_LIMIT),
        name="backward",
    )(source, *([idx] * GB), iq, iqt, hw, grad)


def return_kernel(n_ctx, n_head, pick, dk, out, got_a, part, half, got_b, slots, landed,
                  ra, rb, rc, sa, sb, sc, sx, sp, so):
    me = lax.axis_index("ctx")
    head, x, core, partner = place()
    n_x = n_head // 2
    per = slots.shape[1]
    others = [lax.rem(me + k, n_ctx) for k in range(1, n_ctx)]
    xs = [lax.rem(x + k, n_x) for k in range(1, n_x)]
    greet([{"ctx": o} for o in others] + [{"head": v * 2 + core} for v in xs] + [{"head": partner}])
    pending = []
    order = xs + [x]
    for v in order:
        c = remote(dk.at[v * 2 + 1 - core], got_a.at[v], sa.at[v], ra.at[v], {"head": partner})
        c.start()
        pending.append(c)
    for i, v in enumerate(order):
        remote(got_a.at[v], got_a.at[v], sa.at[v], ra.at[v], {"head": partner}).wait_recv()
        part[v] = dk[v * 2 + core] + got_a[v]
        if i < n_x - 1:
            half[v] = part[v].astype(BF16)
            c = remote(half.at[v], got_b.at[x], sb.at[v], rb.at[x], {"head": v * 2 + core})
            c.start()
            pending.append(c)
    for v in xs:
        remote(got_b.at[v], got_b.at[v], sb.at[v], rb.at[v], {"head": partner}).wait_recv()
        part[x] += got_b[v].astype(F32)

    for i, o in enumerate(others + [me]):
        def fill(k, carry, o=o):
            slots[o, k] = part[x, pick[o, k]].astype(BF16)
            return carry

        lax.fori_loop(0, per, fill, 0)
        if i < n_ctx - 1:
            c = remote(slots.at[o], landed.at[me, head], sc.at[i], rc.at[me, head], {"ctx": o})
            c.start()
            pending.append(c)
    landed[me, head] = slots[me]

    def arrived(o, h):
        remote(landed.at[o, h], landed.at[o, h], sc.at[0], rc.at[o, h], {"head": partner}).wait_recv()

    def send(o, h, sem, to):
        c = remote(landed.at[o, h], landed.at[o, h], sem, rc.at[o, h], {"head": to})
        c.start()
        pending.append(c)

    sources = [me] + [lax.rem(me + n_ctx - k, n_ctx) for k in range(1, n_ctx)]
    for i, o in enumerate(sources):
        if i > 0:
            arrived(o, head)
        for j, v in enumerate(xs):
            send(o, head, sx.at[i, j], v * 2 + core)
        send(o, head, sp.at[i, 0], partner)
    for i, o in enumerate(sources):
        for j, v in enumerate(xs):
            arrived(o, v * 2 + core)
            send(o, v * 2 + core, sp.at[i, 1 + j], partner)
    for i, o in enumerate(sources):
        for v in [x] + xs:
            arrived(o, v * 2 + 1 - core)
    for c in pending:
        c.wait_send()
    c = pltpu.make_async_copy(landed, out, so)
    c.start()
    c.wait()


def give_back(n_ctx, n_head, pick, dk):
    _, u, _, wi = dk.shape
    n_x = n_head // 2
    per = pick.shape[1]
    dma = pltpu.SemaphoreType.DMA
    vm = pl.BlockSpec(memory_space=pltpu.VMEM)
    return pl.pallas_call(
        functools.partial(return_kernel, n_ctx, n_head),
        out_shape=jax.ShapeDtypeStruct((n_ctx, n_head, per, BLK, wi), BF16),
        in_specs=[pl.BlockSpec(memory_space=pltpu.SMEM), vm],
        out_specs=pl.BlockSpec(memory_space=pl.ANY),
        scratch_shapes=[
            pltpu.VMEM((n_x, u, BLK, wi), F32),
            pltpu.VMEM((n_x, u, BLK, wi), F32),
            pltpu.VMEM((n_x, u, BLK, wi), BF16),
            pltpu.VMEM((n_x, u, BLK, wi), BF16),
            pltpu.VMEM((n_ctx, per, BLK, wi), BF16),
            pltpu.VMEM((n_ctx, n_head, per, BLK, wi), BF16),
            dma((n_x,)), dma((n_x,)), dma((n_ctx, n_head)),
            dma((n_x,)), dma((n_x,)), dma((n_ctx,)), dma((n_ctx, n_x)), dma((n_ctx, n_x)),
            dma(()),
        ],
        compiler_params=pltpu.CompilerParams(
            collective_id=2, has_side_effects=True, vmem_limit_bytes=VMEM_LIMIT
        ),
        name="give_back",
    )(pick, dk)


def land_kernel(asked, got, out):
    out[...] = jnp.zeros_like(out)

    def one(f, carry):
        @pl.when(asked[f] >= 0)
        def _():
            out[asked[f]] += got[f].astype(F32)

        return carry

    lax.fori_loop(0, got.shape[0], one, 0)


def land(asked, got, blocks):
    return pl.pallas_call(
        land_kernel,
        out_shape=jax.ShapeDtypeStruct((blocks,) + got.shape[1:], F32),
        in_specs=[pl.BlockSpec(memory_space=pltpu.SMEM), pl.BlockSpec(memory_space=pltpu.VMEM)],
        out_specs=pl.BlockSpec(memory_space=pltpu.VMEM),
        compiler_params=pltpu.CompilerParams(vmem_limit_bytes=VMEM_LIMIT),
        name="land",
    )(asked, got)


def body(
    main_queries,
    latent_keys,
    lse,
    index_queries,
    index_keys,
    head_weights,
    loss_cotangent,
    block_ids,
):
    n_ctx = lax.axis_size("ctx")
    n_head = lax.axis_size("head")
    me = lax.axis_index("ctx")
    head = lax.axis_index("head")
    q, hm, wl = main_queries.shape
    key_rows, wi = index_keys.shape
    ih = index_queries.shape[1]
    owner_blocks = key_rows // BLK
    per = 2 * UB // n_ctx // n_head
    per_head = UB // n_head
    all_blocks = owner_blocks * n_ctx
    n_slot = n_ctx * n_head * per
    blocks = jnp.arange(all_blocks, dtype=jnp.int32)
    present = jnp.any(block_ids.reshape(-1)[:, None] == blocks[None, :], axis=0)
    grid = present.astype(jnp.int32).reshape(n_ctx, owner_blocks)
    count = jnp.sum(grid, axis=1)
    first = jnp.cumsum(count) - count
    inner = jnp.cumsum(grid, axis=1) - 1
    union = (first[:, None] + inner).reshape(-1)
    inner = inner.reshape(-1)
    owner, local = blocks // owner_blocks, blocks % owner_blocks
    klass, turn = union % n_head, inner // n_head
    slot = (owner * n_head + klass) * per + turn
    spot = klass * per_head + union // n_head
    slot_iota = jnp.arange(n_slot, dtype=jnp.int32)
    union_iota = jnp.arange(UB, dtype=jnp.int32)
    in_slot = present[:, None] & (slot[:, None] == slot_iota[None, :])
    in_union = present[:, None] & (spot[:, None] == union_iota[None, :])
    wanted = jnp.max(jnp.where(in_slot, local[:, None], -1), axis=0)
    pick = jnp.max(jnp.where(in_slot, (union // n_head)[:, None], 0), axis=0)
    source = jnp.max(jnp.where(in_union, slot[:, None], 0), axis=0)
    union_block = jnp.max(jnp.where(in_union, blocks[:, None], 0), axis=0)
    asked = lax.all_to_all(
        wanted.reshape(n_ctx, n_head * per), "ctx", split_axis=0, concat_axis=0, tiled=True
    )
    lat_local = latent_keys.reshape(owner_blocks, BLK, wl)
    idx_local = index_keys.reshape(owner_blocks, BLK, wi)
    want3 = wanted.reshape(n_ctx, n_head, per)
    ask3 = asked.reshape(n_ctx, n_head, per)
    mine = jnp.maximum(lax.dynamic_index_in_dim(ask3, head, 1, keepdims=False), 0)
    own = jnp.maximum(lax.dynamic_index_in_dim(want3, me, 0, keepdims=False), 0)
    my_pick = lax.dynamic_index_in_dim(pick.reshape(n_ctx, n_head, per), head, 1, keepdims=False)
    lat_mine, idx_mine, lat_own, idx_own = select(
        mine.reshape(-1), own.reshape(-1), lat_local, idx_local
    )
    lat_got, idx_got = fetch(
        n_ctx,
        n_head,
        lat_mine.reshape(n_ctx, per, BLK, wl),
        idx_mine.reshape(n_ctx, per, BLK, wi),
        lat_own.reshape(n_head, per, BLK, wl),
        idx_own.reshape(n_head, per, BLK, wi),
    )
    lat_got = lat_got.reshape(n_slot, BLK, wl)
    idx_got = idx_got.reshape(n_slot, BLK, wi)
    chosen = jnp.any(union_block[:, None, None] == block_ids[None, :, :], axis=2)
    query_pos = all_blocks * BLK - q * n_ctx + me * q + jnp.arange(q, dtype=jnp.int32)
    lim = jnp.where(chosen, query_pos[None, :] - union_block[:, None] * BLK, -1)
    mq = main_queries.transpose(1, 2, 0)
    iq = index_queries.transpose(1, 0, 2).reshape(ih // 2, 2 * q, wi)
    iqt = iq.transpose(0, 2, 1)
    lse2 = (lse * LOG2E).T.reshape(hm // 2, 2 * q)
    hw2 = head_weights.T.reshape(ih // 2, 2 * q)
    mass, score = forward(source, lat_got, idx_got, mq, lse2, iqt, hw2, lim)
    grad = score_grads(n_head, mass, score, loss_cotangent.reshape(1, q))
    dq, dw, dk = backward(source, idx_got, iq, iqt, hw2, grad)
    d_queries = dq.reshape(ih, q, wi).transpose(1, 0, 2)
    d_weights = dw.reshape(ih, q).T
    back = give_back(n_ctx, n_head, my_pick, dk.reshape(n_head, per_head, BLK, wi))
    d_keys = land(asked.reshape(-1), back.reshape(n_slot, BLK, wi), owner_blocks)
    return (d_queries, d_weights, d_keys.reshape(key_rows, wi))


def solution(mesh):
    placed = (
        P(("grp", "ctx"), "head", None),
        P(("grp", "ctx"), None),
        P(("grp", "ctx"), "head"),
        P(("grp", "ctx"), "head", None),
        P(("grp", "ctx"), None),
        P(("grp", "ctx"), "head"),
        P(("grp", "ctx")),
        P(("grp", "ctx"), None),
    )
    return jax.shard_map(
        body,
        mesh=mesh,
        in_specs=placed,
        out_specs=(
            P(("grp", "ctx"), "head", None),
            P(("grp", "ctx"), "head"),
            P(("grp", "ctx"), None),
        ),
        check_vma=False,
    )
```

```python
import functools
import math

import jax
import jax.numpy as jnp
from jax import lax
from jax.experimental import pallas as pl
from jax.experimental.pallas import tpu as pltpu
from jax.sharding import PartitionSpec as P

BLK = 64
UB = 64
GB = 8
CUTS = 4
AHEAD = 2
ATTN_SCALE = 192.0 ** (-0.5)
LOG2E = math.log2(math.e)
MESH = pl.DeviceIdType.MESH
VMEM_LIMIT = 56 * 1024 * 1024
F32 = jnp.float32
BF16 = jnp.bfloat16


def place():
    head = lax.axis_index("head")
    x, core = head // 2, lax.rem(head, 2)
    return head, x, core, x * 2 + 1 - core


def greet(peers):
    barrier = pltpu.get_barrier_semaphore()
    for peer in peers:
        pl.semaphore_signal(barrier, inc=1, device_id=peer, device_id_type=MESH)
    pl.semaphore_wait(barrier, len(peers))


def remote(src, dst, send, recv, peer):
    return pltpu.make_async_remote_copy(
        src_ref=src, dst_ref=dst, send_sem=send, recv_sem=recv,
        device_id=peer, device_id_type=MESH,
    )


def fetch_kernel(n_ctx, n_head, cuts, lat_mine, idx_mine, lat_own, idx_own, lat_got, idx_got,
                 own_sem, recv_sem, s_ctx, s_x, s_core):
    me = lax.axis_index("ctx")
    head, x, core, partner = place()
    n_x = n_head // 2
    piece = lat_mine.shape[1] // cuts
    others = [lax.rem(me + k, n_ctx) for k in range(1, n_ctx)]
    sources = [lax.rem(me + n_ctx - k, n_ctx) for k in range(1, n_ctx)]
    xs = [lax.rem(x + k, n_x) for k in range(1, n_x)]
    greet([{"ctx": o} for o in others] + [{"head": v * 2 + core} for v in xs] + [{"head": partner}])
    units = range(cuts + 1)

    def mine(a, o):
        return idx_mine.at[o] if a == 0 else lat_mine.at[o, pl.ds((a - 1) * piece, piece)]

    def got(a, o, h):
        return idx_got.at[o, h] if a == 0 else lat_got.at[o, h, pl.ds((a - 1) * piece, piece)]

    pending = []
    def outward(a):
        for i, o in enumerate(others):
            c = remote(mine(a, o), got(a, me, head), s_ctx.at[a, i],
                       recv_sem.at[a, me, head], {"ctx": o})
            c.start()
            pending.append(c)

    for a in units[:AHEAD]:
        outward(a)
    locals_ = [
        pltpu.make_async_copy(idx_own, idx_got.at[me], own_sem.at[0]),
        pltpu.make_async_copy(lat_own, lat_got.at[me], own_sem.at[1]),
    ]
    for c in locals_:
        c.start()

    def arrived(a, o, h):
        remote(got(a, o, h), got(a, o, h), s_core.at[a, 0, 0], recv_sem.at[a, o, h],
               {"head": partner}).wait_recv()

    def send(a, o, h, sem, to):
        c = remote(got(a, o, h), got(a, o, h), sem, recv_sem.at[a, o, h], {"head": to})
        c.start()
        pending.append(c)

    def across(a):
        for i, o in enumerate(sources):
            arrived(a, o, head)
            for j, v in enumerate(xs):
                send(a, o, head, s_x.at[a, i, j], v * 2 + core)
            send(a, o, head, s_core.at[a, i, 0], partner)

    def along(a):
        for i, o in enumerate(sources):
            for j, v in enumerate(xs):
                arrived(a, o, v * 2 + core)
                send(a, o, v * 2 + core, s_core.at[a, i, 1 + j], partner)

    for a in units:
        across(a)
        if a + AHEAD <= cuts:
            outward(a + AHEAD)
        if a > 0:
            along(a - 1)
    along(cuts)
    for a in units:
        for i, o in enumerate(sources):
            for v in [x] + xs:
                arrived(a, o, v * 2 + 1 - core)
    for c in pending:
        c.wait_send()
    for c in locals_:
        c.wait()


def fetch(n_ctx, n_head, lat_mine, idx_mine, lat_own, idx_own):
    per = lat_mine.shape[1]
    n_x = n_head // 2
    cuts = math.gcd(per, CUTS)
    dma = pltpu.SemaphoreType.DMA
    return pl.pallas_call(
        functools.partial(fetch_kernel, n_ctx, n_head, cuts),
        out_shape=(
            jax.ShapeDtypeStruct((n_ctx, n_head) + lat_mine.shape[1:], BF16),
            jax.ShapeDtypeStruct((n_ctx, n_head) + idx_mine.shape[1:], BF16),
        ),
        in_specs=[pl.BlockSpec(memory_space=pl.ANY)] * 2
        + [pl.BlockSpec(memory_space=pltpu.VMEM)] * 2,
        out_specs=(pl.BlockSpec(memory_space=pl.ANY),) * 2,
        scratch_shapes=[
            dma((2,)),
            dma((cuts + 1, n_ctx, n_head)),
            dma((cuts + 1, n_ctx)),
            dma((cuts + 1, n_ctx, n_x)),
            dma((cuts + 1, n_ctx, n_x)),
        ],
        compiler_params=pltpu.CompilerParams(
            collective_id=0, has_side_effects=True, vmem_limit_bytes=VMEM_LIMIT
        ),
        name="fetch",
    )(lat_mine, idx_mine, lat_own, idx_own)


def select_kernel(mine, own, lat, idx, lat_mine, idx_mine, lat_own, idx_own, sem):
    def one(k, carry):
        pltpu.make_async_copy(lat.at[mine[k]], lat_mine.at[k], sem.at[0]).start()
        pltpu.make_async_copy(idx.at[mine[k]], idx_mine.at[k], sem.at[1]).start()
        return carry

    def two(k, carry):
        pltpu.make_async_copy(lat.at[own[k]], lat_own.at[k], sem.at[2]).start()
        pltpu.make_async_copy(idx.at[own[k]], idx_own.at[k], sem.at[3]).start()
        return carry

    lax.fori_loop(0, mine.shape[0], one, 0)
    lax.fori_loop(0, own.shape[0], two, 0)
    for i, r in enumerate((lat_mine, idx_mine, lat_own, idx_own)):
        pltpu.make_async_copy(r, r, sem.at[i]).wait()


def select(mine, own, lat, idx):
    shapes = tuple(
        jax.ShapeDtypeStruct((n,) + a.shape[1:], BF16)
        for n in (mine.shape[0], own.shape[0]) for a in (lat, idx)
    )
    anywhere = pl.BlockSpec(memory_space=pl.ANY)
    return pl.pallas_call(
        select_kernel,
        out_shape=shapes,
        in_specs=[pl.BlockSpec(memory_space=pltpu.SMEM)] * 2 + [anywhere] * 2,
        out_specs=(pl.BlockSpec(memory_space=pltpu.VMEM),) * 4,
        scratch_shapes=[pltpu.SemaphoreType.DMA((4,))],
        compiler_params=pltpu.CompilerParams(vmem_limit_bytes=VMEM_LIMIT),
        name="select",
    )(mine, own, lat, idx)


def forward_kernel(src, *refs):
    lat = refs[:GB]
    idx = refs[GB:2 * GB]
    mq, lse, iq, hw, lim, mass, score, keys, ikeys = refs[2 * GB:]
    q = mass.shape[1]
    wide = lat[0].shape[-1]
    for b in range(GB):
        low, mid, high = b * BLK, b * BLK + BLK // 2, (b + 1) * BLK
        keys[low:high, :wide] = lat[b][0]
        keys[low:mid, wide:] = idx[b][0, BLK:, :BLK]
        keys[mid:high, wide:] = idx[b][0, BLK:, BLK:]
        ikeys[low:high, :] = idx[b][0, :BLK, :]
    mass[...] = jnp.zeros_like(mass)
    score[...] = jnp.zeros_like(score)

    def main(i, carry):
        both = jnp.concatenate([mq[2 * i], mq[2 * i + 1]], axis=1)
        s = jnp.dot(keys[...], both, preferred_element_type=F32)
        e = jnp.exp2(s * (ATTN_SCALE * LOG2E) - lse[pl.ds(i, 1), :])
        mass[...] += e[:, :q] + e[:, q:]
        return carry

    lax.fori_loop(0, mq.shape[0] // 2, main, 0, unroll=True)

    def side(i, carry):
        v = jnp.maximum(jnp.dot(ikeys[...], iq[i], preferred_element_type=F32), 0.0) * hw[pl.ds(i, 1), :]
        score[...] += v[:, :q] + v[:, q:]
        return carry

    lax.fori_loop(0, iq.shape[0], side, 0, unroll=True)
    offset = lax.broadcasted_iota(jnp.int32, (BLK, q), 0)
    for b in range(GB):
        rows = slice(b * BLK, (b + 1) * BLK)
        seen = offset <= lim[b:b + 1, :]
        mass[rows, :] = jnp.where(seen, mass[rows, :], 0.0)
        score[rows, :] = jnp.where(seen, score[rows, :], -1e30)


def slot_specs(array):
    return [
        pl.BlockSpec((1,) + array.shape[1:], lambda g, s, b=b: (s[g * GB + b], 0, 0)) for b in range(GB)
    ]


def forward(source, lat, idx, mq, lse, iq, hw, lim):
    q = lim.shape[1]
    wl, wi = mq.shape[1], idx.shape[-1]
    rows = GB * BLK
    whole = lambda a: pl.BlockSpec(a.shape, lambda g, s, n=a.ndim: (0,) * n)
    return pl.pallas_call(
        forward_kernel,
        grid_spec=pltpu.PrefetchScalarGridSpec(
            num_scalar_prefetch=1,
            grid=(UB // GB,),
            in_specs=slot_specs(lat) + slot_specs(idx) + [whole(mq), whole(lse), whole(iq), whole(hw)]
            + [pl.BlockSpec((GB, q), lambda g, s: (g, 0))],
            out_specs=(pl.BlockSpec((rows, q), lambda g, s: (g, 0)),) * 2,
            scratch_shapes=[pltpu.VMEM((rows, wl), BF16), pltpu.VMEM((rows, wi), BF16)],
        ),
        out_shape=(jax.ShapeDtypeStruct((UB * BLK, q), F32),) * 2,
        compiler_params=pltpu.CompilerParams(vmem_limit_bytes=VMEM_LIMIT),
        name="forward",
    )(source, *([lat] * GB), *([idx] * GB), mq, lse, iq, hw, lim)


def grad_kernel(n_head, mass, score, cot, grad, got_a, part, half, got_s, got_m, stat, whole,
                ra, rb, rs, rg, sa, sb, ss, sg):
    head, x, core, partner = place()
    n_x = n_head // 2
    span = mass.shape[0] // n_head
    xs = [lax.rem(x + k, n_x) for k in range(1, n_x)]
    heads = [lax.rem(head + k, n_head) for k in range(1, n_head)]
    greet([{"head": h} for h in heads])
    rows = lambda h: pl.ds(pl.multiple_of(h * span, span), span)
    both = (score, mass)
    got_b = (got_s, got_m)
    pending = []
    order = xs + [x]
    for v in order:
        for a in range(2):
            c = remote(both[a].at[rows(v * 2 + 1 - core)], got_a.at[a, v], sa.at[a, v],
                       ra.at[a, v], {"head": partner})
            c.start()
            pending.append(c)
    for i, v in enumerate(order):
        for a in range(2):
            remote(got_a.at[a, v], got_a.at[a, v], sa.at[a, v], ra.at[a, v],
                   {"head": partner}).wait_recv()
            part[a, v] = both[a][rows(v * 2 + core), :] + got_a[a, v]
            if i < n_x - 1:
                if a == 1:
                    half[v] = part[1, v].astype(BF16)
                c = remote((part.at[0, v] if a == 0 else half.at[v]), got_b[a].at[x], sb.at[a, v], rb.at[a, x],
                           {"head": v * 2 + core})
                c.start()
                pending.append(c)
    for v in xs:
        for a in range(2):
            remote(got_b[a].at[v], got_b[a].at[v], sb.at[a, v], rb.at[a, v],
                   {"head": partner}).wait_recv()
            part[a, x] += got_b[a][v].astype(F32)
    top = jnp.max(part[0, x], axis=0, keepdims=True)
    expo = jnp.exp(part[0, x] - top)
    stat[head, 0:1, :] = top
    stat[head, 1:2, :] = jnp.sum(expo, axis=0, keepdims=True)
    stat[head, 2:3, :] = jnp.sum(part[1, x], axis=0, keepdims=True)
    stat[head, 3:8, :] = jnp.zeros((5, top.shape[1]), F32)
    for i, h in enumerate(heads):
        c = remote(stat.at[head], stat.at[head], ss.at[i], rs.at[head], {"head": h})
        c.start()
        pending.append(c)
    for h in heads:
        remote(stat.at[h], stat.at[h], ss.at[0], rs.at[h], {"head": partner}).wait_recv()
    best = stat[0, 0:1, :]
    for h in range(1, n_head):
        best = jnp.maximum(best, stat[h, 0:1, :])
    total = jnp.zeros_like(best)
    mass_total = jnp.zeros_like(best)
    for h in range(n_head):
        total += stat[h, 1:2, :] * jnp.exp(stat[h, 0:1, :] - best)
        mass_total += stat[h, 2:3, :]
    left = cot[...] * jnp.exp(top - best) / total
    right = cot[...] / mass_total
    whole[head] = (expo * left - part[1, x] * right).astype(BF16)

    def send(h, sem, to):
        c = remote(whole.at[h], whole.at[h], sem, rg.at[h], {"head": to})
        c.start()
        pending.append(c)

    def arrived(h):
        remote(whole.at[h], whole.at[h], sg.at[0], rg.at[h], {"head": partner}).wait_recv()

    for i, v in enumerate(xs):
        send(head, sg.at[i], v * 2 + core)
    send(head, sg.at[n_x], partner)
    for i, v in enumerate(xs):
        arrived(v * 2 + core)
        send(v * 2 + core, sg.at[n_x + 1 + i], partner)
    for v in [x] + xs:
        arrived(v * 2 + 1 - core)
    for c in pending:
        c.wait_send()
    for h in range(n_head):
        grad[h * span:(h + 1) * span, :] = whole[h]


def score_grads(n_head, mass, score, cot):
    keys, q = mass.shape
    n_x, span = n_head // 2, keys // n_head
    dma = pltpu.SemaphoreType.DMA
    vm = pl.BlockSpec(memory_space=pltpu.VMEM)
    return pl.pallas_call(
        functools.partial(grad_kernel, n_head),
        out_shape=jax.ShapeDtypeStruct((keys, q), BF16),
        in_specs=[vm] * 3,
        out_specs=vm,
        scratch_shapes=[
            pltpu.VMEM((2, n_x, span, q), F32),
            pltpu.VMEM((2, n_x, span, q), F32),
            pltpu.VMEM((n_x, span, q), BF16),
            pltpu.VMEM((n_x, span, q), F32),
            pltpu.VMEM((n_x, span, q), BF16),
            pltpu.VMEM((n_head, 8, q), F32),
            pltpu.VMEM((n_head, span, q), BF16),
            dma((2, n_x)), dma((2, n_x)), dma((n_head,)), dma((n_head,)),
            dma((2, n_x)), dma((2, n_x)), dma((n_head,)), dma((n_head + 1,)),
        ],
        compiler_params=pltpu.CompilerParams(
            collective_id=1, has_side_effects=True, vmem_limit_bytes=VMEM_LIMIT
        ),
        name="score_grads",
    )(mass, score, cot)


def backward_kernel(src, *refs):
    idx = refs[:GB]
    iq, iqt, hw, grad, dq, dw, dk, ikeys, tkeys, acc, gacc = refs[GB:]
    q = grad.shape[1]
    step = pl.program_id(0)

    @pl.when(step == 0)
    def _():
        acc[...] = jnp.zeros_like(acc)
        dw[...] = jnp.zeros_like(dw)

    for b in range(GB):
        ikeys[b * BLK:(b + 1) * BLK, :] = idx[b][0, :BLK, :]
    tkeys[...] = jnp.swapaxes(ikeys[...].astype(F32), 0, 1).astype(BF16)
    gacc[...] = jnp.zeros_like(gacc)

    def one(i, carry):
        pre = jnp.dot(ikeys[...], iqt[i], preferred_element_type=F32)
        half = grad[...].astype(F32)
        g = jnp.concatenate([half, half], axis=1)
        dw[pl.ds(i, 1), :] += jnp.sum(g * jnp.maximum(pre, 0.0), axis=0, keepdims=True)
        pg = jnp.where(pre > 0.0, g * hw[pl.ds(i, 1), :], 0.0).astype(BF16)
        acc[i] += jnp.dot(tkeys[...], pg, preferred_element_type=F32)
        gacc[...] += jnp.dot(pg, iq[i], preferred_element_type=F32)
        return carry

    lax.fori_loop(0, iq.shape[0], one, 0, unroll=True)
    dk[...] = gacc[...]

    @pl.when(step == pl.num_programs(0) - 1)
    def _():
        for i in range(iq.shape[0]):
            dq[i] = jnp.swapaxes(acc[i], 0, 1).astype(BF16)


def backward(source, idx, iq, iqt, hw, grad):
    q = grad.shape[1]
    wi = idx.shape[-1]
    rows = GB * BLK
    pairs = iq.shape[0]
    whole = lambda a: pl.BlockSpec(a.shape, lambda g, s, n=a.ndim: (0,) * n)
    return pl.pallas_call(
        backward_kernel,
        grid_spec=pltpu.PrefetchScalarGridSpec(
            num_scalar_prefetch=1,
            grid=(UB // GB,),
            in_specs=slot_specs(idx) + [whole(iq), whole(iqt), whole(hw), pl.BlockSpec((rows, q), lambda g, s: (g, 0))],
            out_specs=(
                pl.BlockSpec((pairs, 2 * q, wi), lambda g, s: (0, 0, 0)),
                pl.BlockSpec((pairs, 2 * q), lambda g, s: (0, 0)),
                pl.BlockSpec((rows, wi), lambda g, s: (g, 0)),
            ),
            scratch_shapes=[
                pltpu.VMEM((rows, wi), BF16),
                pltpu.VMEM((wi, rows), BF16),
                pltpu.VMEM((pairs, wi, 2 * q), F32),
                pltpu.VMEM((rows, wi), F32),
            ],
        ),
        out_shape=(
            jax.ShapeDtypeStruct((pairs, 2 * q, wi), BF16),
            jax.ShapeDtypeStruct((pairs, 2 * q), F32),
            jax.ShapeDtypeStruct((UB * BLK, wi), F32),
        ),
        compiler_params=pltpu.CompilerParams(vmem_limit_bytes=VMEM_LIMIT),
        name="backward",
    )(source, *([idx] * GB), iq, iqt, hw, grad)


def return_kernel(n_ctx, n_head, pick, dk, out, got_a, part, half, got_b, slots, landed,
                  ra, rb, rc, sa, sb, sc, sx, sp, so):
    me = lax.axis_index("ctx")
    head, x, core, partner = place()
    n_x = n_head // 2
    per = slots.shape[1]
    others = [lax.rem(me + k, n_ctx) for k in range(1, n_ctx)]
    xs = [lax.rem(x + k, n_x) for k in range(1, n_x)]
    greet([{"ctx": o} for o in others] + [{"head": v * 2 + core} for v in xs] + [{"head": partner}])
    pending = []
    order = xs + [x]
    for v in order:
        c = remote(dk.at[v * 2 + 1 - core], got_a.at[v], sa.at[v], ra.at[v], {"head": partner})
        c.start()
        pending.append(c)
    for i, v in enumerate(order):
        remote(got_a.at[v], got_a.at[v], sa.at[v], ra.at[v], {"head": partner}).wait_recv()
        part[v] = dk[v * 2 + core] + got_a[v]
        if i < n_x - 1:
            half[v] = part[v].astype(BF16)
            c = remote(half.at[v], got_b.at[x], sb.at[v], rb.at[x], {"head": v * 2 + core})
            c.start()
            pending.append(c)
    for v in xs:
        remote(got_b.at[v], got_b.at[v], sb.at[v], rb.at[v], {"head": partner}).wait_recv()
        part[x] += got_b[v].astype(F32)

    for i, o in enumerate(others + [me]):
        def fill(k, carry, o=o):
            slots[o, k] = part[x, pick[o, k]].astype(BF16)
            return carry

        lax.fori_loop(0, per, fill, 0)
        if i < n_ctx - 1:
            c = remote(slots.at[o], landed.at[me, head], sc.at[i], rc.at[me, head], {"ctx": o})
            c.start()
            pending.append(c)
    landed[me, head] = slots[me]

    def arrived(o, h):
        remote(landed.at[o, h], landed.at[o, h], sc.at[0], rc.at[o, h], {"head": partner}).wait_recv()

    def send(o, h, sem, to):
        c = remote(landed.at[o, h], landed.at[o, h], sem, rc.at[o, h], {"head": to})
        c.start()
        pending.append(c)

    sources = [me] + [lax.rem(me + n_ctx - k, n_ctx) for k in range(1, n_ctx)]
    for i, o in enumerate(sources):
        if i > 0:
            arrived(o, head)
        for j, v in enumerate(xs):
            send(o, head, sx.at[i, j], v * 2 + core)
        send(o, head, sp.at[i, 0], partner)
    for i, o in enumerate(sources):
        for j, v in enumerate(xs):
            arrived(o, v * 2 + core)
            send(o, v * 2 + core, sp.at[i, 1 + j], partner)
    for i, o in enumerate(sources):
        for v in [x] + xs:
            arrived(o, v * 2 + 1 - core)
    for c in pending:
        c.wait_send()
    c = pltpu.make_async_copy(landed, out, so)
    c.start()
    c.wait()


def give_back(n_ctx, n_head, pick, dk):
    _, u, _, wi = dk.shape
    n_x = n_head // 2
    per = pick.shape[1]
    dma = pltpu.SemaphoreType.DMA
    vm = pl.BlockSpec(memory_space=pltpu.VMEM)
    return pl.pallas_call(
        functools.partial(return_kernel, n_ctx, n_head),
        out_shape=jax.ShapeDtypeStruct((n_ctx, n_head, per, BLK, wi), BF16),
        in_specs=[pl.BlockSpec(memory_space=pltpu.SMEM), vm],
        out_specs=pl.BlockSpec(memory_space=pl.ANY),
        scratch_shapes=[
            pltpu.VMEM((n_x, u, BLK, wi), F32),
            pltpu.VMEM((n_x, u, BLK, wi), F32),
            pltpu.VMEM((n_x, u, BLK, wi), BF16),
            pltpu.VMEM((n_x, u, BLK, wi), BF16),
            pltpu.VMEM((n_ctx, per, BLK, wi), BF16),
            pltpu.VMEM((n_ctx, n_head, per, BLK, wi), BF16),
            dma((n_x,)), dma((n_x,)), dma((n_ctx, n_head)),
            dma((n_x,)), dma((n_x,)), dma((n_ctx,)), dma((n_ctx, n_x)), dma((n_ctx, n_x)),
            dma(()),
        ],
        compiler_params=pltpu.CompilerParams(
            collective_id=2, has_side_effects=True, vmem_limit_bytes=VMEM_LIMIT
        ),
        name="give_back",
    )(pick, dk)


def land_kernel(asked, got, out):
    out[...] = jnp.zeros_like(out)

    def one(f, carry):
        @pl.when(asked[f] >= 0)
        def _():
            out[asked[f]] += got[f].astype(F32)

        return carry

    lax.fori_loop(0, got.shape[0], one, 0)


def land(asked, got, blocks):
    return pl.pallas_call(
        land_kernel,
        out_shape=jax.ShapeDtypeStruct((blocks,) + got.shape[1:], F32),
        in_specs=[pl.BlockSpec(memory_space=pltpu.SMEM), pl.BlockSpec(memory_space=pltpu.VMEM)],
        out_specs=pl.BlockSpec(memory_space=pltpu.VMEM),
        compiler_params=pltpu.CompilerParams(vmem_limit_bytes=VMEM_LIMIT),
        name="land",
    )(asked, got)


def body(
    main_queries,
    latent_keys,
    lse,
    index_queries,
    index_keys,
    head_weights,
    loss_cotangent,
    block_ids,
):
    n_ctx = lax.axis_size("ctx")
    n_head = lax.axis_size("head")
    me = lax.axis_index("ctx")
    head = lax.axis_index("head")
    q, hm, wl = main_queries.shape
    key_rows, wi = index_keys.shape
    ih = index_queries.shape[1]
    owner_blocks = key_rows // BLK
    per = 2 * UB // n_ctx // n_head
    per_head = UB // n_head
    all_blocks = owner_blocks * n_ctx
    n_slot = n_ctx * n_head * per
    blocks = jnp.arange(all_blocks, dtype=jnp.int32)
    present = jnp.any(block_ids.reshape(-1)[:, None] == blocks[None, :], axis=0)
    grid = present.astype(jnp.int32).reshape(n_ctx, owner_blocks)
    count = jnp.sum(grid, axis=1)
    first = jnp.cumsum(count) - count
    inner = jnp.cumsum(grid, axis=1) - 1
    union = (first[:, None] + inner).reshape(-1)
    inner = inner.reshape(-1)
    owner, local = blocks // owner_blocks, blocks % owner_blocks
    klass, turn = union % n_head, inner // n_head
    slot = (owner * n_head + klass) * per + turn
    spot = klass * per_head + union // n_head
    slot_iota = jnp.arange(n_slot, dtype=jnp.int32)
    union_iota = jnp.arange(UB, dtype=jnp.int32)
    in_slot = present[:, None] & (slot[:, None] == slot_iota[None, :])
    in_union = present[:, None] & (spot[:, None] == union_iota[None, :])
    wanted = jnp.max(jnp.where(in_slot, local[:, None], -1), axis=0)
    pick = jnp.max(jnp.where(in_slot, (union // n_head)[:, None], 0), axis=0)
    source = jnp.max(jnp.where(in_union, slot[:, None], 0), axis=0)
    union_block = jnp.max(jnp.where(in_union, blocks[:, None], 0), axis=0)
    asked = lax.all_to_all(
        wanted.reshape(n_ctx, n_head * per), "ctx", split_axis=0, concat_axis=0, tiled=True
    )
    wide = wl - BLK
    lat_local = latent_keys[:, :wide].reshape(owner_blocks, BLK, wide)
    tail = latent_keys[:, wide:].reshape(owner_blocks, 2, BLK // 2, BLK).transpose(0, 2, 1, 3)
    idx_local = jnp.concatenate(
        [index_keys.reshape(owner_blocks, BLK, wi), tail.reshape(owner_blocks, BLK // 2, 2 * BLK)],
        axis=1,
    )
    want3 = wanted.reshape(n_ctx, n_head, per)
    ask3 = asked.reshape(n_ctx, n_head, per)
    mine = jnp.maximum(lax.dynamic_index_in_dim(ask3, head, 1, keepdims=False), 0)
    own = jnp.maximum(lax.dynamic_index_in_dim(want3, me, 0, keepdims=False), 0)
    my_pick = lax.dynamic_index_in_dim(pick.reshape(n_ctx, n_head, per), head, 1, keepdims=False)
    lat_mine, idx_mine, lat_own, idx_own = select(
        mine.reshape(-1), own.reshape(-1), lat_local, idx_local
    )
    lat_got, idx_got = fetch(
        n_ctx,
        n_head,
        lat_mine.reshape((n_ctx, per) + lat_mine.shape[1:]),
        idx_mine.reshape((n_ctx, per) + idx_mine.shape[1:]),
        lat_own.reshape((n_head, per) + lat_own.shape[1:]),
        idx_own.reshape((n_head, per) + idx_own.shape[1:]),
    )
    lat_got = lat_got.reshape((n_slot,) + lat_got.shape[3:])
    idx_got = idx_got.reshape((n_slot,) + idx_got.shape[3:])
    chosen = jnp.any(union_block[:, None, None] == block_ids[None, :, :], axis=2)
    query_pos = all_blocks * BLK - q * n_ctx + me * q + jnp.arange(q, dtype=jnp.int32)
    lim = jnp.where(chosen, query_pos[None, :] - union_block[:, None] * BLK, -1)
    mq = main_queries.transpose(1, 2, 0)
    iq = index_queries.transpose(1, 0, 2).reshape(ih // 2, 2 * q, wi)
    iqt = iq.transpose(0, 2, 1)
    lse2 = (lse * LOG2E).T.reshape(hm // 2, 2 * q)
    hw2 = head_weights.T.reshape(ih // 2, 2 * q)
    mass, score = forward(source, lat_got, idx_got, mq, lse2, iqt, hw2, lim)
    grad = score_grads(n_head, mass, score, loss_cotangent.reshape(1, q))
    dq, dw, dk = backward(source, idx_got, iq, iqt, hw2, grad)
    d_queries = dq.reshape(ih, q, wi).transpose(1, 0, 2)
    d_weights = dw.reshape(ih, q).T
    back = give_back(n_ctx, n_head, my_pick, dk.reshape(n_head, per_head, BLK, wi))
    d_keys = land(asked.reshape(-1), back.reshape(n_slot, BLK, wi), owner_blocks)
    return (d_queries, d_weights, d_keys.reshape(key_rows, wi))


def solution(mesh):
    placed = (
        P(("grp", "ctx"), "head", None),
        P(("grp", "ctx"), None),
        P(("grp", "ctx"), "head"),
        P(("grp", "ctx"), "head", None),
        P(("grp", "ctx"), None),
        P(("grp", "ctx"), "head"),
        P(("grp", "ctx")),
        P(("grp", "ctx"), None),
    )
    return jax.shard_map(
        body,
        mesh=mesh,
        in_specs=placed,
        out_specs=(
            P(("grp", "ctx"), "head", None),
            P(("grp", "ctx"), "head"),
            P(("grp", "ctx"), None),
        ),
        check_vma=False,
    )
```
